512 devices in a mesh: panel: 16 (over z_lo, x), tile: 32 (over y, z_hi, core).
Axes of the slice: x: 4, y: 8, z: 8 (z_hi: 2, z_lo: 4; z = z_hi * 4 + z_lo), core: 2. Of those that a mesh axis runs over, the one named last changes fastest.
Arguments:
- snapshots: bfloat16 [128, 256, 2, 512], P('panel', 'tile'), may hold values from -24 to 24
- beam_codes: int32 [32, 256], P(None, 'tile'), may hold values from 0 to 63
- panel_codes: int32 [128], replicated, may hold values from 0 to 63
- loading: float32 [128], P('panel'), may hold values from 1 to 10
Outputs:
- cancel: float32 [128, 62, 2], P('panel')
- beam_out: float32 [2, 512], P(None, 'tile')
The draws below stay inside these ranges and needn't reach their ends.
All inputs are finite; a program needn't handle non-finite values.
Results may differ from the reference program's by a relative error of at most 0.0036.
Values may be sent and summed in bfloat16 or wider, within the bound.
No kernel may reach another device: no remote copies, remote signals or barrier semaphores. Data moves between devices by JAX's collectives and lax.ppermute only.
A program may use at most 64 MiB of HBM per device.

```python
import math
import jax
import jax.numpy as jnp
from jax import lax

BEAMS = 32
SNAPS = 512
INTERFERERS = 40
PANELS = 128
TILES = 256


def draw_snapshots(key, part):
    key_dir, key_amp, key_sig, key_noise = jax.random.split(jax.random.fold_in(key, 17), 4)
    elements = PANELS * TILES
    direction = jax.random.uniform(key_dir, (INTERFERERS,), minval=-1.0, maxval=1.0)
    amplitude = jax.random.uniform(key_amp, (INTERFERERS,), minval=0.2, maxval=0.6)
    position = jnp.arange(elements, dtype=jnp.float32)
    phase = jnp.pi * direction[:, None] * position[None, :]
    along_real = jnp.cos(phase)
    along_imag = jnp.sin(phase)
    signal = jax.random.normal(key_sig, (2, INTERFERERS, SNAPS), jnp.float32) * amplitude[None, :, None]
    real_part = jnp.dot(along_real.T, signal[0], precision=lax.Precision.HIGHEST) - jnp.dot(along_imag.T, signal[1], precision=lax.Precision.HIGHEST)
    imag_part = jnp.dot(along_imag.T, signal[0], precision=lax.Precision.HIGHEST) + jnp.dot(along_real.T, signal[1], precision=lax.Precision.HIGHEST)
    noise = jax.random.normal(key_noise, (elements, 2, SNAPS), jnp.float32)
    values = jnp.stack([real_part, imag_part], axis=1) + noise
    values = jnp.clip(values, -24.0, 24.0)
    return values.reshape(PANELS, TILES, 2, SNAPS).astype(jnp.bfloat16)


def plant(drawn, key, least, top_value):
    longest = drawn.shape.index(max(drawn.shape))
    spots = []
    for shift in (0, 1):
        where = [jax.random.randint(jax.random.fold_in(key, axis), (), 0, length) for axis, length in enumerate(drawn.shape)]
        where[longest] = (where[longest] + shift) % drawn.shape[longest]
        spots.append(tuple(where))
    return drawn.at[spots[0]].set(least).at[spots[1]].set(top_value)


def shard_levels(own_key, dims, cuts, least, largest):
    gain = 1.0
    for dim, blocks in cuts:
        heights = jax.random.uniform(jax.random.fold_in(jax.random.fold_in(own_key, 6), dim), (blocks,), jnp.float32, least / len(cuts), largest / len(cuts))
        gain = gain * jnp.repeat(jnp.exp(heights), dims[dim] // blocks).reshape((-1,) + (1,) * (len(dims) - 1 - dim))
    return gain


def setup_inputs(seed: int = 0) -> dict:
    splits = jax.random.split(jax.random.key(seed), 5)
    return {
        "snapshots": draw_snapshots(jax.random.fold_in(splits[4], 71), 0),
        "beam_codes": plant(jax.random.randint(splits[1], (BEAMS, TILES), 0, 64), jax.random.fold_in(splits[1], 1), 0, 63).astype(jnp.int32),
        "panel_codes": plant(jax.random.randint(splits[2], (PANELS,), 0, 64), jax.random.fold_in(splits[2], 1), 0, 63).astype(jnp.int32),
        "loading": jnp.clip(jnp.exp(math.log(10.0) - 2.3025851 * jax.random.uniform(splits[3], (PANELS,), jnp.float32) ** shard_levels(splits[3], (PANELS,), ((0, 16),), -0.2, 0.2)), 1.0, 10.0),
    }


phase_levels = 64
array_load = 1.0

def steering_rows(codes, total_tiles):
    angles = codes.astype(jnp.float32) * (2.0 * math.pi / phase_levels)
    cosine = jnp.cos(angles)
    sine = jnp.sin(angles)
    count_beams = codes.shape[0]
    count_tiles = codes.shape[1]
    real_rows = jnp.stack([cosine, sine], axis=-1).reshape(count_beams, 2 * count_tiles)
    imag_rows = jnp.stack([-sine, cosine], axis=-1).reshape(count_beams, 2 * count_tiles)
    table = jnp.stack([real_rows, imag_rows], axis=1).reshape(2 * count_beams, 2 * count_tiles)
    return (table / math.sqrt(total_tiles)).astype(jnp.bfloat16)

def solve_one(factor_one, right_one):
    return jax.scipy.linalg.cho_solve((factor_one, True), right_one)

def cancel_weights(covar):
    factor = jnp.linalg.cholesky(covar[:, 2:, 2:])
    return jax.vmap(solve_one)(factor, covar[:, 2:, :2])

def constraint_matrix(panel_codes):
    angles = panel_codes.astype(jnp.float32) * (2.0 * math.pi / phase_levels)
    cosine = jnp.cos(angles)
    sine = jnp.sin(angles)
    upper = jnp.stack([cosine, -sine], axis=-1)
    lower = jnp.stack([sine, cosine], axis=-1)
    return jnp.stack([upper, lower], axis=1).reshape(2 * panel_codes.shape[0], 2)

def array_weights(covar, constraint):
    factor = jnp.linalg.cholesky(covar)
    solved = jax.scipy.linalg.cho_solve((factor, True), constraint)
    gram = jnp.dot(constraint.T, solved, precision=lax.Precision.HIGHEST)
    determinant = gram[0, 0] * gram[1, 1] - gram[0, 1] * gram[1, 0]
    inverse = jnp.stack([jnp.stack([gram[1, 1], -gram[0, 1]]), jnp.stack([-gram[1, 0], gram[0, 0]])]) / determinant
    return jnp.dot(solved, inverse, precision=lax.Precision.HIGHEST)

def reference(snapshots, beam_codes, panel_codes, loading):
    table = steering_rows(beam_codes, TILES)
    samples = snapshots.reshape(PANELS, 2 * TILES, SNAPS).astype(jnp.float32)
    beams = jnp.einsum('bk,pks->pbs', table.astype(jnp.float32), samples, precision=lax.Precision.HIGHEST)
    width = 2 * BEAMS
    covar = jnp.einsum('pis,pjs->pij', beams, beams, precision=lax.Precision.HIGHEST) / SNAPS
    covar = covar + loading[:, None, None] * jnp.eye(width, dtype=jnp.float32)[None, :, :]
    cancel = cancel_weights(covar)
    outputs = beams[:, :2, :] - jnp.einsum('pak,pas->pks', cancel, beams[:, 2:, :], precision=lax.Precision.HIGHEST)
    flat = outputs.reshape(2 * PANELS, SNAPS)
    array_covar = jnp.dot(flat, flat.T, precision=lax.Precision.HIGHEST) / SNAPS
    array_covar = array_covar + array_load * jnp.eye(2 * PANELS, dtype=jnp.float32)
    weights = array_weights(array_covar, constraint_matrix(panel_codes))
    beam_out = jnp.dot(weights.T, flat, precision=lax.Precision.HIGHEST) * math.sqrt(PANELS)
    return (cancel, beam_out)
```

```python
import math

import jax
import jax.numpy as jnp
from jax import lax
from jax.experimental import pallas as pl
from jax.experimental.pallas import tpu as pltpu
from jax.sharding import Mesh
from jax.sharding import PartitionSpec as P

SNAPS = 512
PHASE_LEVELS = 64
ARRAY_LOAD = 1.0
TILE = ("tile_y", "tile_z", "core")
BLOCK = 64
HIGHEST = lax.Precision.HIGHEST


def vmem():
    return pl.BlockSpec(memory_space=pltpu.VMEM)


def smem():
    return pl.BlockSpec(memory_space=pltpu.SMEM)


def lanes_of(block, lane):
    return jnp.broadcast_to(block[:, lane : lane + 1], (8, 128))


def row_of(block, row):
    return jnp.broadcast_to(block[row : row + 1, :], (8, 128))


def eliminate(rows, first_lane, steps):
    rows = [list(row) for row in rows]
    place = lax.broadcasted_iota(jnp.int32, (8, 128), 0)
    for k in range(0, steps, 2):
        own, s = divmod(k, 8)
        lane = first_lane + k
        upper = [row_of(group, s) for group in rows[own]]
        lower = [row_of(group, s + 1) for group in rows[own]]
        left = [lanes_of(row[0], lane) for row in rows]
        right = [lanes_of(row[0], lane + 1) for row in rows]
        a = row_of(left[own], s)
        b = row_of(right[own], s)
        c = row_of(right[own], s + 1)
        scale = 1.0 / (a * c - b * b)
        a, b, c = a * scale, b * scale, c * scale
        for i, row in enumerate(rows):
            f0 = c * left[i] - b * right[i]
            f1 = a * right[i] - b * left[i]
            for g in range(len(row)):
                value = row[g] - f0 * upper[g] - f1 * lower[g]
                if i == own:
                    value = jnp.where(place == s, c * upper[g] - b * lower[g], value)
                    value = jnp.where(place == s + 1, a * lower[g] - b * upper[g], value)
                row[g] = value
    return rows


def beams_kernel(got_ref, beams_ref, covar_ref):
    got = got_ref[...]
    pieces = got[:, 32:40, :].astype(jnp.float32)
    table = jnp.concatenate([pieces, pltpu.roll(pieces, 64, 2)], axis=1)
    table = table.reshape(512, 128).astype(jnp.bfloat16)
    samples = jnp.concatenate(
        [got[:, 0:16, :].reshape(512, 128), got[:, 16:32, :].reshape(512, 128)], axis=1
    )
    beams = lax.dot_general(
        table, samples, (((0,), (0,)), ((), ())), preferred_element_type=jnp.float32
    )[:64]
    beams_ref[...] = beams
    covar_ref[...] = lax.dot_general(
        beams, beams, (((1,), (1,)), ((), ())), precision=HIGHEST, preferred_element_type=jnp.float32
    )


def cancel_kernel(loading_ref, place_ref, beams_ref, own_ref, other_ref, out_ref):
    load = loading_ref[place_ref[0]]
    covar = (own_ref[...] + other_ref[...]) / SNAPS
    row = lax.broadcasted_iota(jnp.int32, (64, 64), 0)
    column = lax.broadcasted_iota(jnp.int32, (64, 64), 1)
    covar = covar + jnp.where(row == column, load, 0.0)
    covar = jnp.concatenate([covar, jnp.zeros((64, 64), jnp.float32)], axis=1)
    solved = eliminate([[covar[8 * i : 8 * i + 8, :]] for i in range(8)], 0, 62)
    whole = jnp.concatenate([row[0] for row in solved], axis=0)
    whole = jnp.concatenate([whole, jnp.zeros((64, 128), jnp.float32)], axis=0)
    turned = whole.T[62:64, :]
    lane = lax.broadcasted_iota(jnp.int32, (2, 128), 1)
    turned = jnp.where(lane < 62, turned, 0.0)
    beams = beams_ref[...]
    outputs = beams[62:64, :] - jnp.dot(
        turned[:, :64], beams, precision=HIGHEST, preferred_element_type=jnp.float32
    )
    out_ref[0:2, :] = outputs[:, 0:128]
    out_ref[2:4, :] = outputs[:, 128:256]
    lane = lax.broadcasted_iota(jnp.int32, (1, 128), 1)
    out_ref[4:5, :] = jnp.where(lane < 64, turned[0:1, :], pltpu.roll(turned, 64, 1)[1:2, :])


def array_kernel(place_ref, codes_ref, own_ref, other_ref, cancel_ref, out_ref, work_ref):
    y = place_ref[0]
    slot = place_ref[1]
    core = place_ref[2]
    panel = place_ref[3]
    cancel_ref[...] = own_ref[pl.ds(panel * 40 + 4, 8, stride=5), :]

    def block(ref, k, b):
        return ref[pl.ds(2 * b + k, 128, stride=5), :]

    def half(ref):
        return jnp.concatenate(
            [
                jnp.concatenate([block(ref, k, 0), block(ref, k, 1)], axis=1)
                for k in range(2)
            ],
            axis=0,
        )

    def square(flat):
        return lax.dot_general(
            flat, flat, (((1,), (1,)), ((), ())), precision=HIGHEST, preferred_element_type=jnp.float32
        )

    own = half(own_ref)
    other = half(other_ref)
    row = lax.broadcasted_iota(jnp.int32, (256, 256), 0)
    column = lax.broadcasted_iota(jnp.int32, (256, 256), 1)
    covar = (square(own) + square(other)) / SNAPS + jnp.where(row == column, ARRAY_LOAD, 0.0)

    angles = codes_ref[...].astype(jnp.float32) * (2.0 * math.pi / PHASE_LEVELS)
    cosine = jnp.cos(angles)
    sine = jnp.sin(angles)
    spread_cosine = jnp.broadcast_to(cosine, (128, 128)).T
    spread_sine = jnp.broadcast_to(sine, (128, 128)).T

    mine = jnp.where(core == y // 4, own, other)
    mine = jnp.where((y % 4) // 2 == 0, mine[:, :128], mine[:, 128:])
    mine = pltpu.roll(mine, lax.rem(128 - 16 * slot, 128), 1)
    lane = lax.broadcasted_iota(jnp.int32, (128, 128), 1)

    def right_side(values, first, second):
        values = jnp.where(lane < 16, values, 0.0)
        return jnp.where(lane == 16, first, jnp.where(lane == 17, second, values))

    work_ref[0:256, 0:256] = covar
    work_ref[0:128, 256:384] = right_side(mine[:128], spread_cosine, -spread_sine)
    work_ref[128:256, 256:384] = right_side(mine[128:], spread_sine, spread_cosine)
    work_ref[256:264, :] = jnp.zeros((8, 384), jnp.float32)
    work_ref[256:257, 0:128] = cosine
    work_ref[256:257, 128:256] = sine
    work_ref[257:258, 0:128] = -sine
    work_ref[257:258, 128:256] = cosine

    for start in range(0, 256, BLOCK):
        stop = start + BLOCK
        first = start // 128
        groups = list(range(first, 3))
        rows = [
            [work_ref[r : r + 8, 128 * g : 128 * g + 128] for g in groups]
            for r in range(start, stop, 8)
        ]
        rows = eliminate(rows, start % 128, BLOCK)
        if stop % 128 == 0:
            groups, rows = groups[1:], [row[1:] for row in rows]
        solved = jnp.concatenate([jnp.concatenate(row, axis=1) for row in rows], axis=0)
        lines = [solved]
        width = solved.shape[1]
        before, after = start % 128, 128 - start % 128 - BLOCK
        if before:
            lines = [jnp.zeros((before, width), jnp.float32)] + lines
        if after:
            lines = lines + [jnp.zeros((after, width), jnp.float32)]
        solved = jnp.concatenate(lines, axis=0) if len(lines) > 1 else solved
        cuts = [(stop, stop + BLOCK), (stop + BLOCK, 264)] if stop < 256 else [(256, 264)]
        left = 128 * groups[0]
        for top, bottom in cuts:
            if top >= bottom:
                continue
            factor = work_ref[top:bottom, 128 * first : 128 * first + 128]
            work_ref[top:bottom, left:384] = work_ref[top:bottom, left:384] - jnp.dot(
                factor, solved, precision=HIGHEST, preferred_element_type=jnp.float32
            )

    final = -work_ref[256:264, 256:384]
    upper = row_of(final, 0)
    lower = row_of(final, 1)
    g00 = lanes_of(upper, 16)
    g01 = lanes_of(upper, 17)
    g10 = lanes_of(lower, 16)
    g11 = lanes_of(lower, 17)
    scale = math.sqrt(128.0) / (g00 * g11 - g01 * g10)
    first_row = (g11 * upper - g10 * lower) * scale
    second_row = (g00 * lower - g01 * upper) * scale
    place = lax.broadcasted_iota(jnp.int32, (8, 128), 0)
    out_ref[...] = jnp.where(place == 0, first_row, second_row)[0:2, 0:16]


def steering_columns(codes):
    angles = codes.T.astype(jnp.float32) * (2.0 * math.pi / PHASE_LEVELS)
    cosine = jnp.cos(angles)
    sine = jnp.sin(angles)
    real = jnp.stack([cosine, -sine], axis=-1)
    imag = jnp.stack([sine, cosine], axis=-1)
    tiles, beams = angles.shape
    table = jnp.stack([real, imag], axis=1).reshape(2 * tiles, 2 * beams)
    table = (table / math.sqrt(256)).astype(jnp.bfloat16)
    return jnp.concatenate([table[:, 2:], table[:, :2]], axis=1)


def body(snapshots, beam_codes, panel_codes, loading):
    y = lax.axis_index("tile_y")
    z = lax.axis_index("tile_z")
    core = lax.axis_index("core")
    panel = lax.axis_index("panel")
    table = steering_columns(beam_codes)
    table = jnp.concatenate([table[:8], table[8:]], axis=1)
    samples = snapshots.reshape(8, 16, 2, 2, 128)
    samples = samples.transpose(0, 2, 3, 1, 4).reshape(8, 2, 32, 128)
    table = jnp.broadcast_to(table[None, None], (8, 2, 8, 128))
    message = jnp.concatenate([samples, table], axis=2)
    message = jnp.broadcast_to(message[:, None], (8, 2, 2, 40, 128)).reshape(32, 40, 128)
    got = lax.all_to_all(message, TILE, 0, 0, tiled=True)
    beams, covar = pl.pallas_call(
        beams_kernel,
        out_shape=(
            jax.ShapeDtypeStruct((64, 256), jnp.float32),
            jax.ShapeDtypeStruct((64, 64), jnp.float32),
        ),
        in_specs=[vmem()],
        out_specs=(vmem(), vmem()),
        name="beams",
    )(got)
    other = lax.ppermute(covar, "core", [(0, 1), (1, 0)])
    line = pl.pallas_call(
        cancel_kernel,
        out_shape=jax.ShapeDtypeStruct((5, 128), jnp.float32),
        in_specs=[smem(), smem(), vmem(), vmem(), vmem()],
        out_specs=vmem(),
        name="cancel",
    )(loading, y.reshape(1), beams, covar, other)
    lines = jnp.broadcast_to(line.reshape(1, 5, 1, 128), (128, 5, 1, 128))
    gathered = lax.all_to_all(lines, ("panel", "tile_y"), 0, 0, tiled=True)
    gathered = gathered.reshape(640, 128)
    other = lax.ppermute(gathered, "core", [(0, 1), (1, 0)])
    slot = (y % 2) * 4 + z * 2 + core
    place = jnp.stack([y, slot, core, panel]).astype(jnp.int32)
    cancel, beam_out = pl.pallas_call(
        array_kernel,
        out_shape=(
            jax.ShapeDtypeStruct((8, 128), jnp.float32),
            jax.ShapeDtypeStruct((2, 16), jnp.float32),
        ),
        in_specs=[smem(), vmem(), vmem(), vmem()],
        out_specs=(vmem(), vmem()),
        scratch_shapes=[pltpu.VMEM((264, 384), jnp.float32)],
        name="array",
    )(place, panel_codes.reshape(1, 128), gathered, other)
    cancel = cancel.reshape(8, 2, 64)[:, :, :62].transpose(0, 2, 1)
    return cancel, beam_out


def solution(mesh):
    torus = Mesh(
        mesh.devices.reshape(mesh.shape["panel"], 8, 2, 2), ("panel", "tile_y", "tile_z", "core")
    )
    return jax.shard_map(
        body,
        mesh=torus,
        in_specs=(P("panel", TILE, None, None), P(None, TILE), P(), P("panel")),
        out_specs=(P("panel", None, None), P(None, TILE)),
        check_vma=False,
    )
```

```python
import math

import jax
import jax.numpy as jnp
from jax import lax
from jax.experimental import pallas as pl
from jax.experimental.pallas import tpu as pltpu
from jax.sharding import Mesh
from jax.sharding import PartitionSpec as P

SNAPS = 512
PHASE_LEVELS = 64
ARRAY_LOAD = 1.0
TILE = ("tile_y", "tile_z", "core")
BLOCK = 32
CHUNK = 8
HIGHEST = lax.Precision.HIGHEST


def vmem():
    return pl.BlockSpec(memory_space=pltpu.VMEM)


def smem():
    return pl.BlockSpec(memory_space=pltpu.SMEM)


def limit(mebibytes):
    return pltpu.CompilerParams(vmem_limit_bytes=mebibytes << 20)


def lanes_of(block, lane):
    return jnp.broadcast_to(block[:, lane : lane + 1], (8, 128))


def row_of(block, row):
    return jnp.broadcast_to(block[row : row + 1, :], (8, 128))


def eliminate(rows, first_lane, steps):
    rows = [list(row) for row in rows]
    place = lax.broadcasted_iota(jnp.int32, (8, 128), 0)
    for first in range(0, steps, CHUNK):
        count = min(CHUNK, steps - first)
        spread = [[lanes_of(row[0], first_lane + first + u) for u in range(count)] for row in rows]
        for t in range(count):
            own, s = divmod(first + t, 8)
            scale = 1.0 / row_of(spread[own][t], s)
            lead = {u: row_of(spread[own][u], s) for u in range(t + 1, count)}
            upper = [row_of(group, s) for group in rows[own]]
            for i, row in enumerate(rows):
                f = spread[i][t]
                if i == own:
                    for u in lead:
                        value = spread[i][u] - (f * lead[u]) * scale
                        spread[i][u] = jnp.where(place == s, lead[u] * scale, value)
                    for g in range(len(row)):
                        value = row[g] - (f * upper[g]) * scale
                        row[g] = jnp.where(place == s, upper[g] * scale, value)
                else:
                    f = f * scale
                    for u in lead:
                        spread[i][u] = spread[i][u] - f * lead[u]
                    for g in range(len(row)):
                        row[g] = row[g] - f * upper[g]
    return rows


def cosine_of(steps):
    quarter = (steps + 8) >> 4
    angle = (steps - 16 * quarter).astype(jnp.float32) * (2.0 * math.pi / PHASE_LEVELS)
    square = angle * angle
    cosine = 1.0 + square * (
        -1 / 2 + square * (1 / 24 + square * (-1 / 720 + square * (1 / 40320 - square / 3628800)))
    )
    sine = angle * (
        1.0 + square * (-1 / 6 + square * (1 / 120 + square * (-1 / 5040 + square / 362880)))
    )
    value = jnp.where((quarter & 1) == 0, cosine, sine)
    return jnp.where(((quarter + 1) & 2) == 0, value, -value)


def message_kernel(samples_ref, codes_ref, out_ref):
    codes = jnp.concatenate([codes_ref[...], jnp.zeros((8, 96), jnp.int32)], axis=1)
    row = lax.broadcasted_iota(jnp.int32, (8, 128), 0)
    lane = lax.broadcasted_iota(jnp.int32, (8, 128), 1)
    column = lane & 63

    def placed(values, offset):
        real = pltpu.roll(values, (offset + 127) % 128, 1)
        imag = pltpu.roll(values, offset + 30, 1)
        last = pltpu.roll(values, offset + 62, 1)
        twin = pltpu.roll(values, offset + 63, 1)
        values = jnp.where(column < 31, real, jnp.where(column < 62, imag, last))
        return jnp.where(column == 63, twin, values)

    def doubled(values, first):
        result = row_of(values, first)
        for t in range(1, 4):
            result = jnp.where(row >= 2 * t, row_of(values, first + t), result)
        return result

    spread = jnp.where(lane < 64, doubled(placed(codes, 0), 0), doubled(placed(codes, 64), 4))
    imaginary = jnp.where((column >= 31) & (column != 62), 1, 0)
    table = cosine_of(spread + 16 * (imaginary - (row & 1)))
    table = (table / math.sqrt(256)).astype(jnp.bfloat16)
    for p in range(8):
        for c in range(2):
            for b in range(2):
                start = 256 * c + 128 * b
                value = samples_ref[p, :, start : start + 128]
                for z in range(2):
                    out_ref[4 * p + 2 * z + c, 16 * b : 16 * b + 16, :] = value
            for z in range(2):
                out_ref[4 * p + 2 * z + c, 32:40, :] = table


def beams_kernel(got_ref, beams_ref, covar_ref):
    got = got_ref[...]
    pieces = got[:, 32:40, :].astype(jnp.float32)
    table = jnp.concatenate([pieces, pltpu.roll(pieces, 64, 2)], axis=1)
    table = table.reshape(512, 128).astype(jnp.bfloat16)
    samples = jnp.concatenate(
        [got[:, 0:16, :].reshape(512, 128), got[:, 16:32, :].reshape(512, 128)], axis=1
    )
    beams = lax.dot_general(
        table, samples, (((0,), (0,)), ((), ())), preferred_element_type=jnp.float32
    )[:64]
    beams_ref[...] = beams
    covar_ref[...] = lax.dot_general(
        beams, beams, (((1,), (1,)), ((), ())), precision=HIGHEST, preferred_element_type=jnp.float32
    )


def cancel_kernel(loading_ref, beams_ref, own_ref, other_ref, out_ref):
    load = loading_ref[lax.axis_index("tile_y")]
    covar = (own_ref[...] + other_ref[...]) / SNAPS
    row = lax.broadcasted_iota(jnp.int32, (64, 64), 0)
    column = lax.broadcasted_iota(jnp.int32, (64, 64), 1)
    covar = covar + jnp.where(row == column, load, 0.0)
    covar = jnp.concatenate([covar, jnp.zeros((64, 64), jnp.float32)], axis=1)
    solved = eliminate([[covar[8 * i : 8 * i + 8, :]] for i in range(8)], 0, 62)
    whole = jnp.concatenate([row[0] for row in solved], axis=0)
    whole = jnp.concatenate([whole, jnp.zeros((64, 128), jnp.float32)], axis=0)
    turned = whole.T[62:64, :]
    lane = lax.broadcasted_iota(jnp.int32, (2, 128), 1)
    turned = jnp.where(lane < 62, turned, 0.0)[:, :64]
    beams = beams_ref[...]
    outputs = beams[62:64, :] - jnp.dot(
        turned, beams, precision=HIGHEST, preferred_element_type=jnp.float32
    )
    row = lax.broadcasted_iota(jnp.int32, (64, 64), 0)
    column = lax.broadcasted_iota(jnp.int32, (64, 64), 1)
    source = jnp.where(column < 62, column // 2 + 31 * (column & 1), column)
    paired = jnp.dot(
        turned,
        jnp.where(row == source, 1.0, 0.0),
        precision=HIGHEST,
        preferred_element_type=jnp.float32,
    )
    line = jnp.concatenate(
        [
            outputs[:, 0:128],
            outputs[:, 128:256],
            jnp.concatenate([paired[0:1, :], paired[1:2, :]], axis=1),
        ],
        axis=0,
    )
    for i in range(8):
        out_ref[5 * i : 5 * i + 5, :] = line
    lines = out_ref[0:40, :]
    for i in range(1, 16):
        out_ref[40 * i : 40 * i + 40, :] = lines


def array_kernel(codes_ref, own_ref, other_ref, cancel_ref, out_ref, work_ref):
    y = lax.axis_index("tile_y")
    core = lax.axis_index("core")
    slot = (y % 2) * 4 + lax.axis_index("tile_z") * 2 + core
    cancel = own_ref[pl.ds(lax.axis_index("panel") * 40 + 4, 8, stride=5), :]
    cancel_ref[:, 0, :] = cancel[:, :62]
    cancel_ref[:, 1, :] = pltpu.roll(cancel, 64, 1)[:, :62]

    def block(ref, k, b):
        return ref[pl.ds(2 * b + k, 128, stride=5), :]

    def half(ref):
        return jnp.concatenate(
            [
                jnp.concatenate([block(ref, k, 0), block(ref, k, 1)], axis=1)
                for k in range(2)
            ],
            axis=0,
        )

    def square(flat):
        return lax.dot_general(
            flat, flat, (((1,), (1,)), ((), ())), precision=HIGHEST, preferred_element_type=jnp.float32
        )

    own = half(own_ref)
    other = half(other_ref)
    row = lax.broadcasted_iota(jnp.int32, (256, 256), 0)
    column = lax.broadcasted_iota(jnp.int32, (256, 256), 1)
    covar = (square(own) + square(other)) / SNAPS + jnp.where(row == column, ARRAY_LOAD, 0.0)

    cosine = cosine_of(codes_ref[...])
    sine = cosine_of(codes_ref[...] - 16)
    spread_cosine = jnp.broadcast_to(cosine, (128, 128)).T
    spread_sine = jnp.broadcast_to(sine, (128, 128)).T

    mine = jnp.where(core == y // 4, own, other)
    mine = jnp.where((y % 4) // 2 == 0, mine[:, :128], mine[:, 128:])
    mine = pltpu.roll(mine, lax.rem(128 - 16 * slot, 128), 1)
    lane = lax.broadcasted_iota(jnp.int32, (128, 128), 1)

    def right_side(values, first, second):
        values = jnp.where(lane < 16, values, 0.0)
        return jnp.where(lane == 16, first, jnp.where(lane == 17, second, values))

    work_ref[0:256, 0:256] = covar
    work_ref[0:128, 256:384] = right_side(mine[:128], spread_cosine, -spread_sine)
    work_ref[128:256, 256:384] = right_side(mine[128:], spread_sine, spread_cosine)
    work_ref[256:264, :] = jnp.zeros((8, 384), jnp.float32)
    work_ref[256:257, 0:128] = cosine
    work_ref[256:257, 128:256] = sine
    work_ref[257:258, 0:128] = -sine
    work_ref[257:258, 128:256] = cosine

    for start in range(0, 256, BLOCK):
        stop = start + BLOCK
        first = start // 128
        groups = list(range(first, 3))
        rows = [
            [work_ref[r : r + 8, 128 * g : 128 * g + 128] for g in groups]
            for r in range(start, stop, 8)
        ]
        rows = eliminate(rows, start % 128, BLOCK)
        if stop % 128 == 0:
            groups, rows = groups[1:], [row[1:] for row in rows]
        solved = jnp.concatenate([jnp.concatenate(row, axis=1) for row in rows], axis=0)
        lines = [solved]
        width = solved.shape[1]
        before, after = start % 128, 128 - start % 128 - BLOCK
        if before:
            lines = [jnp.zeros((before, width), jnp.float32)] + lines
        if after:
            lines = lines + [jnp.zeros((after, width), jnp.float32)]
        solved = jnp.concatenate(lines, axis=0) if len(lines) > 1 else solved
        cuts = [(stop, stop + BLOCK), (stop + BLOCK, 264)] if stop < 256 else [(256, 264)]
        left = 128 * groups[0]
        for top, bottom in cuts:
            if top >= bottom:
                continue
            factor = work_ref[top:bottom, 128 * first : 128 * first + 128]
            work_ref[top:bottom, left:384] = work_ref[top:bottom, left:384] - jnp.dot(
                factor, solved, precision=HIGHEST, preferred_element_type=jnp.float32
            )

    final = -work_ref[256:264, 256:384]
    upper = row_of(final, 0)
    lower = row_of(final, 1)
    g00 = lanes_of(upper, 16)
    g01 = lanes_of(upper, 17)
    g10 = lanes_of(lower, 16)
    g11 = lanes_of(lower, 17)
    scale = math.sqrt(128.0) / (g00 * g11 - g01 * g10)
    first_row = (g11 * upper - g10 * lower) * scale
    second_row = (g00 * lower - g01 * upper) * scale
    place = lax.broadcasted_iota(jnp.int32, (8, 128), 0)
    out_ref[...] = jnp.where(place == 0, first_row, second_row)[0:2, 0:16]


def body(snapshots, beam_codes, panel_codes, loading):
    message = pl.pallas_call(
        message_kernel,
        out_shape=jax.ShapeDtypeStruct((32, 40, 128), jnp.bfloat16),
        in_specs=[vmem(), vmem()],
        out_specs=vmem(),
        compiler_params=limit(4),
        name="message",
    )(snapshots.reshape(8, 16, SNAPS), beam_codes.T)
    got = lax.all_to_all(message, TILE, 0, 0, tiled=True)
    beams, covar = pl.pallas_call(
        beams_kernel,
        out_shape=(
            jax.ShapeDtypeStruct((64, 256), jnp.float32),
            jax.ShapeDtypeStruct((64, 64), jnp.float32),
        ),
        in_specs=[vmem()],
        out_specs=(vmem(), vmem()),
        compiler_params=limit(4),
        name="beams",
    )(got)
    other = lax.ppermute(covar, "core", [(0, 1), (1, 0)])
    lines = pl.pallas_call(
        cancel_kernel,
        out_shape=jax.ShapeDtypeStruct((640, 128), jnp.float32),
        in_specs=[smem(), vmem(), vmem(), vmem()],
        out_specs=vmem(),
        compiler_params=limit(4),
        name="cancel",
    )(loading, beams, covar, other)
    lines = lines.reshape(128, 5, 1, 128)
    gathered = lax.all_to_all(lines, ("panel", "tile_y"), 0, 0, tiled=True)
    gathered = gathered.reshape(640, 128)
    other = lax.ppermute(gathered, "core", [(0, 1), (1, 0)])
    cancel, beam_out = pl.pallas_call(
        array_kernel,
        out_shape=(
            jax.ShapeDtypeStruct((8, 2, 62), jnp.float32),
            jax.ShapeDtypeStruct((2, 16), jnp.float32),
        ),
        in_specs=[vmem(), vmem(), vmem()],
        out_specs=(vmem(), vmem()),
        scratch_shapes=[pltpu.VMEM((264, 384), jnp.float32)],
        compiler_params=limit(8),
        name="array",
    )(panel_codes.reshape(1, 128), gathered, other)
    return cancel.transpose(0, 2, 1), beam_out


def solution(mesh):
    torus = Mesh(
        mesh.devices.reshape(mesh.shape["panel"], 8, 2, 2), ("panel", "tile_y", "tile_z", "core")
    )
    return jax.shard_map(
        body,
        mesh=torus,
        in_specs=(P("panel", TILE, None, None), P(None, TILE), P(), P("panel")),
        out_specs=(P("panel", None, None), P(None, TILE)),
        check_vma=False,
    )
```

```python
import math

import jax
import jax.numpy as jnp
from jax import lax
from jax.experimental import pallas as pl
from jax.experimental.pallas import tpu as pltpu
from jax.sharding import Mesh
from jax.sharding import PartitionSpec as P

SNAPS = 512
PHASE_LEVELS = 64
ARRAY_LOAD = 1.0
TILE = ("tile_y", "tile_z", "core")
CHUNK = 16
NEAR = 16
HIGHEST = lax.Precision.HIGHEST


def vmem():
    return pl.BlockSpec(memory_space=pltpu.VMEM)


def smem():
    return pl.BlockSpec(memory_space=pltpu.SMEM)


def limit(mebibytes):
    return pltpu.CompilerParams(vmem_limit_bytes=mebibytes << 20)


def lanes_of(block, lane):
    return jnp.broadcast_to(block[:, lane : lane + 1], (8, 128))


def row_of(block, row):
    return jnp.broadcast_to(block[row : row + 1, :], (8, 128))


def eliminate(rows, first_lane, steps):
    rows = [list(row) for row in rows]
    place = lax.broadcasted_iota(jnp.int32, (8, 128), 0)
    for first in range(0, steps, CHUNK):
        count = min(CHUNK, steps - first)
        spread = [[lanes_of(row[0], first_lane + first + u) for u in range(count)] for row in rows]
        for t in range(count):
            own, s = divmod(first + t, 8)
            scale = 1.0 / row_of(spread[own][t], s)
            lead = {u: row_of(spread[own][u], s) for u in range(t + 1, count)}
            upper = [row_of(group, s) for group in rows[own]]
            for i, row in enumerate(rows):
                f = spread[i][t]
                if i == own:
                    for u in lead:
                        line = lead[u] * scale
                        if u == t + 1:
                            value = spread[i][u] - (f * lead[u]) * scale
                        else:
                            value = spread[i][u] - f * line
                        spread[i][u] = jnp.where(place == s, line, value)
                    for g in range(len(row)):
                        line = upper[g] * scale
                        row[g] = jnp.where(place == s, line, row[g] - f * line)
                else:
                    f = f * scale
                    for u in lead:
                        spread[i][u] = spread[i][u] - f * lead[u]
                    for g in range(len(row)):
                        row[g] = row[g] - f * upper[g]
    return rows


def less_product(value, spread, lines):
    terms = [f * line for f, line in zip(spread, lines)]
    while len(terms) > 1:
        terms = [sum(terms[i : i + 2]) for i in range(0, len(terms), 2)]
    return value - terms[0]


def forward(rows, steps):
    rows = [list(row) for row in rows]
    for first in range(0, steps, CHUNK):
        count = min(CHUNK, steps - first)
        own = range(first // 8, (first + count + 7) // 8)
        below = range(own.stop, len(rows))
        spread = {i: [lanes_of(rows[i][0], first + t) for t in range(count)] for i in below}
        solved = eliminate([rows[i] for i in own], first, count)
        for i, row in zip(own, solved):
            rows[i] = row
        for g in range(len(rows[0])):
            lines = [row_of(solved[t // 8][g], t % 8) for t in range(count)]
            for i in below:
                rows[i][g] = less_product(rows[i][g], spread[i], lines)
    return rows


def cosine_of(steps):
    quarter = (steps + 8) >> 4
    angle = (steps - 16 * quarter).astype(jnp.float32) * (2.0 * math.pi / PHASE_LEVELS)
    square = angle * angle
    cosine = 1.0 + square * (
        -1 / 2 + square * (1 / 24 + square * (-1 / 720 + square * (1 / 40320 - square / 3628800)))
    )
    sine = angle * (
        1.0 + square * (-1 / 6 + square * (1 / 120 + square * (-1 / 5040 + square / 362880)))
    )
    value = jnp.where((quarter & 1) == 0, cosine, sine)
    return jnp.where(((quarter + 1) & 2) == 0, value, -value)


def message_kernel(samples_ref, codes_ref, out_ref):
    codes = jnp.concatenate([codes_ref[...], jnp.zeros((8, 96), jnp.int32)], axis=1)
    row = lax.broadcasted_iota(jnp.int32, (8, 128), 0)
    lane = lax.broadcasted_iota(jnp.int32, (8, 128), 1)
    real = pltpu.roll(codes, 127, 1)
    imag = pltpu.roll(codes, 30, 1)
    last = pltpu.roll(codes, 62, 1)
    twin = pltpu.roll(codes, 63, 1)
    codes = jnp.where(lane < 31, real, jnp.where(lane < 62, imag, last))
    codes = jnp.where(lane == 63, twin, codes)
    imaginary = jnp.where((lane >= 31) & (lane != 62), 1, 0)

    def columns(first):
        spread = row_of(codes, first)
        for t in range(1, 4):
            spread = jnp.where(row >= 2 * t, row_of(codes, first + t), spread)
        return cosine_of(spread + 16 * (imaginary - (row & 1)))

    table = jnp.concatenate([columns(0), columns(4)], axis=0)
    table = (table / math.sqrt(256)).astype(jnp.bfloat16)
    for p in range(8):
        for z in range(2):
            for b in range(4):
                out_ref[2 * p + z, 16 * b : 16 * b + 16, :] = samples_ref[
                    p, :, 128 * b : 128 * b + 128
                ]
            out_ref[2 * p + z, 64:80, :] = table


def beams_kernel(got_ref, beams_ref):
    got = got_ref[...]
    table = got[:, 64:80, :].reshape(256, 128)
    samples = jnp.concatenate(
        [got[:, 16 * b : 16 * b + 16, :].reshape(256, 128) for b in range(4)], axis=1
    )
    beams_ref[...] = lax.dot_general(
        table, samples, (((0,), (0,)), ((), ())), preferred_element_type=jnp.float32
    )[:64]


def cancel_kernel(loading_ref, own_ref, other_ref, out_ref):
    load = loading_ref[lax.axis_index("tile_y")]
    core = lax.axis_index("core")
    beams = own_ref[...] + other_ref[...]
    covar = square(beams) / SNAPS
    row = lax.broadcasted_iota(jnp.int32, (64, 64), 0)
    column = lax.broadcasted_iota(jnp.int32, (64, 64), 1)
    covar = covar + jnp.where(row == column, load, 0.0)
    covar = jnp.concatenate([covar, jnp.zeros((64, 64), jnp.float32)], axis=1)
    half = jnp.where(core == 0, beams[:, :256], beams[:, 256:])
    row = lax.broadcasted_iota(jnp.int32, (64, 128), 0)
    column = lax.broadcasted_iota(jnp.int32, (64, 128), 1) & 63
    source = jnp.where(column < 62, column // 2 + 31 * (column & 1), 64)
    identity = jnp.where(row == source, 1.0, 0.0)
    whole = jnp.concatenate([covar, half, identity], axis=1)
    rows = [
        [whole[8 * i : 8 * i + 8, 128 * g : 128 * g + 128] for g in range(4)] for i in range(8)
    ]
    last = forward(rows, 62)[7]
    lane = lax.broadcasted_iota(jnp.int32, (1, 128), 1)
    cancel = jnp.where(lane < 64, -last[3][6:7, :], -last[3][7:8, :])
    line = jnp.concatenate([last[1][6:8, :], last[2][6:8, :], cancel], axis=0)
    for i in range(8):
        out_ref[5 * i : 5 * i + 5, :] = line
    lines = out_ref[0:40, :]
    for i in range(1, 16):
        out_ref[40 * i : 40 * i + 40, :] = lines


def square(value):
    return lax.dot_general(
        value,
        value,
        (((1,), (1,)), ((), ())),
        precision=HIGHEST,
        preferred_element_type=jnp.float32,
    )


def flat_half(ref):
    return jnp.concatenate(
        [
            jnp.concatenate(
                [ref[pl.ds(2 * b + k, 128, stride=5), :] for b in range(2)], axis=1
            )
            for k in range(2)
        ],
        axis=0,
    )


def own_columns(flat, half):
    y = lax.axis_index("tile_y")
    slot = (y % 2) * 4 + lax.axis_index("tile_z") * 2 + lax.axis_index("core")
    mine = jnp.where((y % 4) // 2 == 0, flat[:, :128], flat[:, 128:])
    mine = pltpu.roll(mine, lax.rem(128 - 16 * slot, 128), 1)
    lane = lax.broadcasted_iota(jnp.int32, (256, 128), 1)
    return jnp.where((lane < 16) & (half == y // 4), mine, 0.0)


def own_kernel(codes_ref, own_ref, cancel_ref, out_ref):
    cancel = own_ref[pl.ds(lax.axis_index("panel") * 40 + 4, 8, stride=5), :]
    cancel_ref[:, 0, :] = cancel[:, :62]
    cancel_ref[:, 1, :] = pltpu.roll(cancel, 64, 1)[:, :62]
    own = flat_half(own_ref)
    row = lax.broadcasted_iota(jnp.int32, (256, 256), 0)
    column = lax.broadcasted_iota(jnp.int32, (256, 256), 1)
    out_ref[0:256, 0:256] = square(own) / SNAPS + jnp.where(row == column, ARRAY_LOAD, 0.0)
    cosine = cosine_of(codes_ref[...])
    sine = cosine_of(codes_ref[...] - 16)
    spread_cosine = jnp.broadcast_to(cosine, (128, 128)).T
    spread_sine = jnp.broadcast_to(sine, (128, 128)).T
    mine = own_columns(own, lax.axis_index("core"))
    lane = lax.broadcasted_iota(jnp.int32, (128, 128), 1)

    def right_side(values, first, second):
        return jnp.where(lane == 16, first, jnp.where(lane == 17, second, values))

    out_ref[0:128, 256:384] = right_side(mine[:128], spread_cosine, -spread_sine)
    out_ref[128:256, 256:384] = right_side(mine[128:], spread_sine, spread_cosine)
    out_ref[256:264, :] = jnp.zeros((8, 384), jnp.float32)
    out_ref[256:257, 0:128] = cosine
    out_ref[256:257, 128:256] = sine
    out_ref[257:258, 0:128] = -sine
    out_ref[257:258, 128:256] = cosine


def array_kernel(start_ref, other_ref, out_ref, work_ref):
    other = flat_half(other_ref)
    work_ref[0:256, 0:256] = start_ref[0:256, 0:256] + square(other) / SNAPS
    work_ref[0:256, 256:384] = start_ref[0:256, 256:384] + own_columns(
        other, 1 - lax.axis_index("core")
    )
    work_ref[256:264, :] = start_ref[256:264, :]

    for base in range(0, 256, CHUNK):
        stop = base + CHUNK
        first = base // 128
        lane = base % 128
        groups = list(range(first, 3))
        after = list(range(stop // 128, 3))
        near = min(stop + NEAR, 264) if stop < 256 else 264
        rows = [
            [work_ref[r : r + 8, 128 * g : 128 * g + 128] for g in groups]
            for r in range(base, stop, 8)
        ]
        spread = {
            r: [
                lanes_of(work_ref[r : r + 8, 128 * first : 128 * first + 128], lane + t)
                for t in range(CHUNK)
            ]
            for r in range(stop, near, 8)
        }
        rows = eliminate(rows, lane, CHUNK)
        rows = [[row[g - first] for g in after] for row in rows]
        for i, g in enumerate(after):
            lines = [row_of(rows[t // 8][i], t % 8) for t in range(CHUNK)]
            span = slice(128 * g, 128 * g + 128)
            for r in range(stop, near, 8):
                work_ref[r : r + 8, span] = less_product(work_ref[r : r + 8, span], spread[r], lines)
        if near < 264:
            left = 128 * after[0]
            parts = [jnp.concatenate(row, axis=1) for row in rows]
            if lane:
                parts = [jnp.zeros((lane, 384 - left), jnp.float32)] + parts
            if lane + CHUNK < 128:
                parts = parts + [jnp.zeros((128 - lane - CHUNK, 384 - left), jnp.float32)]
            factor = work_ref[near:264, 128 * first : 128 * first + 128]
            work_ref[near:264, left:384] = work_ref[near:264, left:384] - jnp.dot(
                factor,
                jnp.concatenate(parts, axis=0),
                precision=HIGHEST,
                preferred_element_type=jnp.float32,
            )

    final = -work_ref[256:264, 256:384]
    upper = row_of(final, 0)
    lower = row_of(final, 1)
    g00 = lanes_of(upper, 16)
    g01 = lanes_of(upper, 17)
    g10 = lanes_of(lower, 16)
    g11 = lanes_of(lower, 17)
    scale = math.sqrt(128.0) / (g00 * g11 - g01 * g10)
    first_row = (g11 * upper - g10 * lower) * scale
    second_row = (g00 * lower - g01 * upper) * scale
    place = lax.broadcasted_iota(jnp.int32, (8, 128), 0)
    out_ref[...] = jnp.where(place == 0, first_row, second_row)[0:2, 0:16]


def body(snapshots, beam_codes, panel_codes, loading):
    message = pl.pallas_call(
        message_kernel,
        out_shape=jax.ShapeDtypeStruct((16, 80, 128), jnp.bfloat16),
        in_specs=[vmem(), vmem()],
        out_specs=vmem(),
        compiler_params=limit(4),
        name="message",
    )(snapshots.reshape(8, 16, SNAPS), beam_codes.T)
    got = lax.all_to_all(message, ("tile_y", "tile_z"), 0, 0, tiled=True)
    beams = pl.pallas_call(
        beams_kernel,
        out_shape=jax.ShapeDtypeStruct((64, SNAPS), jnp.float32),
        in_specs=[vmem()],
        out_specs=vmem(),
        compiler_params=limit(4),
        name="beams",
    )(got)
    other = lax.ppermute(beams, "core", [(0, 1), (1, 0)])
    lines = pl.pallas_call(
        cancel_kernel,
        out_shape=jax.ShapeDtypeStruct((640, 128), jnp.float32),
        in_specs=[smem(), vmem(), vmem()],
        out_specs=vmem(),
        compiler_params=limit(4),
        name="cancel",
    )(loading, beams, other)
    lines = lines.reshape(128, 5, 1, 128)
    gathered = lax.all_to_all(lines, ("panel", "tile_y"), 0, 0, tiled=True)
    gathered = gathered.reshape(640, 128)
    other = lax.ppermute(gathered, "core", [(0, 1), (1, 0)])
    cancel, start = pl.pallas_call(
        own_kernel,
        out_shape=(
            jax.ShapeDtypeStruct((8, 2, 62), jnp.float32),
            jax.ShapeDtypeStruct((264, 384), jnp.float32),
        ),
        in_specs=[vmem(), vmem()],
        out_specs=(vmem(), vmem()),
        compiler_params=limit(8),
        cost_estimate=pl.CostEstimate(flops=400000000, bytes_accessed=800000, transcendentals=0),
        name="own",
    )(panel_codes.reshape(1, 128), gathered)
    beam_out = pl.pallas_call(
        array_kernel,
        out_shape=jax.ShapeDtypeStruct((2, 16), jnp.float32),
        in_specs=[vmem(), vmem()],
        out_specs=vmem(),
        scratch_shapes=[pltpu.VMEM((264, 384), jnp.float32)],
        compiler_params=limit(8),
        name="array",
    )(start, other)
    return cancel.transpose(0, 2, 1), beam_out


def solution(mesh):
    torus = Mesh(
        mesh.devices.reshape(mesh.shape["panel"], 8, 2, 2), ("panel", "tile_y", "tile_z", "core")
    )
    return jax.shard_map(
        body,
        mesh=torus,
        in_specs=(P("panel", TILE, None, None), P(None, TILE), P(), P("panel")),
        out_specs=(P("panel", None, None), P(None, TILE)),
        check_vma=False,
    )
```

```python
import math

import jax
import jax.numpy as jnp
from jax import lax
from jax.experimental import pallas as pl
from jax.experimental.pallas import tpu as pltpu
from jax.sharding import Mesh
from jax.sharding import PartitionSpec as P

SNAPS = 512
PHASE_LEVELS = 64
ARRAY_LOAD = 1.0
TILE = ("tile_y", "tile_z", "core")
CHUNK = 16
NEAR = 16
MOVE = 32
ROWS = 272
HIGHEST = lax.Precision.HIGHEST


def vmem():
    return pl.BlockSpec(memory_space=pltpu.VMEM)


def smem():
    return pl.BlockSpec(memory_space=pltpu.SMEM)


def limit(mebibytes):
    return pltpu.CompilerParams(vmem_limit_bytes=mebibytes << 20)


def lanes_of(block, lane):
    return jnp.broadcast_to(block[:, lane : lane + 1], (8, 128))


def row_of(block, row):
    return jnp.broadcast_to(block[row : row + 1, :], (8, 128))


def eliminate(rows, first_lane, steps):
    rows = [list(row) for row in rows]
    place = lax.broadcasted_iota(jnp.int32, (8, 128), 0)
    spread = [[lanes_of(row[0], first_lane + u) for u in range(steps)] for row in rows]
    same = [jnp.ones((8, 128), jnp.float32) for row in rows]
    twin = [jnp.zeros((8, 128), jnp.float32) for row in rows]
    for t in range(0, steps, 2):
        own, s = divmod(t, 8)
        a = row_of(spread[own][t], s)
        b = row_of(spread[own][t + 1], s)
        c = row_of(spread[own][t + 1], s + 1)
        scale = 1.0 / (a * c - b * b)
        raw = (a, b, c)
        a, b, c = a * scale, b * scale, c * scale
        pair = (place == s) | (place == s + 1)
        same[own] = jnp.where(place == s, c, jnp.where(place == s + 1, a, same[own]))
        twin[own] = jnp.where(pair, -b, twin[own])
        first = [c * row[t] - b * row[t + 1] for row in spread]
        second = [a * row[t + 1] - b * row[t] for row in spread]
        first[own] = jnp.where(pair, 0.0, first[own])
        second[own] = jnp.where(pair, 0.0, second[own])

        def reduce(blocks):
            upper = row_of(blocks[own], s)
            lower = row_of(blocks[own], s + 1)
            return [
                block - (f * upper + h * lower) for block, f, h in zip(blocks, first, second)
            ]

        for u in range(t + 2, steps):
            quick = None
            if u < t + 4:
                target = (t + 2) // 8
                upper = row_of(spread[own][u], s)
                lower = row_of(spread[own][u], s + 1)
                block = spread[target]
                f = raw[2] * block[t] - raw[1] * block[t + 1]
                h = raw[0] * block[t + 1] - raw[1] * block[t]
                change = f * upper + h * lower
                if target == own:
                    change = jnp.where(pair, 0.0, change)
                quick = block[u] - change * scale
            for row, value in zip(spread, reduce([row[u] for row in spread])):
                row[u] = value
            if quick is not None:
                spread[target][u] = quick
        for g in range(len(rows[0])):
            for row, value in zip(rows, reduce([row[g] for row in rows])):
                row[g] = value

    def scaled(value, i):
        lines = [row_of(value, s ^ 1) for s in range(8)]
        for step in (1, 2, 4):
            lines = [
                jnp.where((place & step) == 0, lines[2 * j], lines[2 * j + 1])
                for j in range(len(lines) // 2)
            ]
        swapped = lines[0]
        return value * same[i] + swapped * twin[i]

    return [[scaled(value, i) for value in row] for i, row in enumerate(rows)]


def less_product(value, spread, lines):
    terms = [f * line for f, line in zip(spread, lines)]
    while len(terms) > 1:
        terms = [sum(terms[i : i + 2]) for i in range(0, len(terms), 2)]
    return value - terms[0]


def forward(rows, steps):
    rows = [list(row) for row in rows]
    for first in range(0, steps, CHUNK):
        count = min(CHUNK, steps - first)
        own = range(first // 8, (first + count + 7) // 8)
        below = range(own.stop, len(rows))
        spread = {i: [lanes_of(rows[i][0], first + t) for t in range(count)] for i in below}
        solved = eliminate([rows[i] for i in own], first, count)
        for i, row in zip(own, solved):
            rows[i] = row
        for g in range(len(rows[0])):
            lines = [row_of(solved[t // 8][g], t % 8) for t in range(count)]
            for i in below:
                rows[i][g] = less_product(rows[i][g], spread[i], lines)
    return rows


def cosine_of(steps):
    quarter = (steps + 8) >> 4
    angle = (steps - 16 * quarter).astype(jnp.float32) * (2.0 * math.pi / PHASE_LEVELS)
    square = angle * angle
    cosine = 1.0 + square * (
        -1 / 2 + square * (1 / 24 + square * (-1 / 720 + square * (1 / 40320 - square / 3628800)))
    )
    sine = angle * (
        1.0 + square * (-1 / 6 + square * (1 / 120 + square * (-1 / 5040 + square / 362880)))
    )
    value = jnp.where((quarter & 1) == 0, cosine, sine)
    return jnp.where(((quarter + 1) & 2) == 0, value, -value)


def message_kernel(samples_ref, codes_ref, out_ref):
    codes = jnp.concatenate([codes_ref[...], jnp.zeros((8, 96), jnp.int32)], axis=1)
    row = lax.broadcasted_iota(jnp.int32, (8, 128), 0)
    lane = lax.broadcasted_iota(jnp.int32, (8, 128), 1)
    real = pltpu.roll(codes, 127, 1)
    imag = pltpu.roll(codes, 30, 1)
    last = pltpu.roll(codes, 62, 1)
    twin = pltpu.roll(codes, 63, 1)
    codes = jnp.where(lane < 31, real, jnp.where(lane < 62, imag, last))
    codes = jnp.where(lane == 63, twin, codes)
    imaginary = jnp.where((lane >= 31) & (lane != 62), 1, 0)

    def columns(first):
        spread = row_of(codes, first)
        for t in range(1, 4):
            spread = jnp.where(row >= 2 * t, row_of(codes, first + t), spread)
        return cosine_of(spread + 16 * (imaginary - (row & 1)))

    table = jnp.concatenate([columns(0), columns(4)], axis=0)
    table = (table / math.sqrt(256)).astype(jnp.bfloat16)
    for p in range(8):
        for z in range(2):
            for b in range(4):
                out_ref[2 * p + z, 16 * b : 16 * b + 16, :] = samples_ref[
                    p, :, 128 * b : 128 * b + 128
                ]
            out_ref[2 * p + z, 64:80, :] = table


def beams_kernel(got_ref, beams_ref):
    got = got_ref[...]
    table = got[:, 64:80, :].reshape(256, 128)
    samples = jnp.concatenate(
        [got[:, 16 * b : 16 * b + 16, :].reshape(256, 128) for b in range(4)], axis=1
    )
    beams_ref[...] = lax.dot_general(
        table, samples, (((0,), (0,)), ((), ())), preferred_element_type=jnp.float32
    )[:64]


def cancel_kernel(loading_ref, own_ref, other_ref, out_ref):
    load = loading_ref[lax.axis_index("tile_y")]
    core = lax.axis_index("core")
    beams = own_ref[...] + other_ref[...]
    covar = square(beams) / SNAPS
    row = lax.broadcasted_iota(jnp.int32, (64, 64), 0)
    column = lax.broadcasted_iota(jnp.int32, (64, 64), 1)
    covar = covar + jnp.where(row == column, load, 0.0)
    covar = jnp.concatenate([covar, jnp.zeros((64, 64), jnp.float32)], axis=1)
    half = jnp.where(core == 0, beams[:, :256], beams[:, 256:])
    row = lax.broadcasted_iota(jnp.int32, (64, 128), 0)
    column = lax.broadcasted_iota(jnp.int32, (64, 128), 1) & 63
    source = jnp.where(column < 62, column // 2 + 31 * (column & 1), 64)
    identity = jnp.where(row == source, 1.0, 0.0)
    whole = jnp.concatenate([covar, half, identity], axis=1)
    rows = [
        [whole[8 * i : 8 * i + 8, 128 * g : 128 * g + 128] for g in range(4)] for i in range(8)
    ]
    last = forward(rows, 62)[7]
    lane = lax.broadcasted_iota(jnp.int32, (1, 128), 1)
    cancel = jnp.where(lane < 64, -last[3][6:7, :], -last[3][7:8, :])
    line = jnp.concatenate([last[1][6:8, :], last[2][6:8, :], cancel], axis=0)
    for i in range(8):
        out_ref[5 * i : 5 * i + 5, :] = line
    lines = out_ref[0:40, :]
    for i in range(1, 16):
        out_ref[40 * i : 40 * i + 40, :] = lines


def square(value):
    return lax.dot_general(
        value,
        value,
        (((1,), (1,)), ((), ())),
        precision=HIGHEST,
        preferred_element_type=jnp.float32,
    )


def flat_half(ref):
    return jnp.concatenate(
        [
            jnp.concatenate(
                [ref[pl.ds(2 * b + k, 128, stride=5), :] for b in range(2)], axis=1
            )
            for k in range(2)
        ],
        axis=0,
    )


def own_columns(flat, half):
    y = lax.axis_index("tile_y")
    slot = (y % 2) * 4 + lax.axis_index("tile_z") * 2 + lax.axis_index("core")
    mine = jnp.where((y % 4) // 2 == 0, flat[:, :128], flat[:, 128:])
    mine = pltpu.roll(mine, lax.rem(128 - 16 * slot, 128), 1)
    lane = lax.broadcasted_iota(jnp.int32, (256, 128), 1)
    return jnp.where((lane < 16) & (half == y // 4), mine, 0.0)


def own_kernel(codes_ref, own_ref, cancel_ref, out_ref):
    cancel = own_ref[pl.ds(lax.axis_index("panel") * 40 + 4, 8, stride=5), :]
    cancel_ref[:, 0, :] = cancel[:, :62]
    cancel_ref[:, 1, :] = pltpu.roll(cancel, 64, 1)[:, :62]
    own = flat_half(own_ref)
    row = lax.broadcasted_iota(jnp.int32, (256, 256), 0)
    column = lax.broadcasted_iota(jnp.int32, (256, 256), 1)
    out_ref[0:256, 0:256] = square(own) / SNAPS + jnp.where(row == column, ARRAY_LOAD, 0.0)
    cosine = cosine_of(codes_ref[...])
    sine = cosine_of(codes_ref[...] - 16)
    spread_cosine = jnp.broadcast_to(cosine, (128, 128)).T
    spread_sine = jnp.broadcast_to(sine, (128, 128)).T
    mine = own_columns(own, lax.axis_index("core"))
    lane = lax.broadcasted_iota(jnp.int32, (128, 128), 1)

    def right_side(values, first, second):
        return jnp.where(lane == 16, first, jnp.where(lane == 17, second, values))

    out_ref[0:128, 256:384] = right_side(mine[:128], spread_cosine, -spread_sine)
    out_ref[128:256, 256:384] = right_side(mine[128:], spread_sine, spread_cosine)
    out_ref[256:264, :] = jnp.zeros((8, 384), jnp.float32)
    out_ref[256:257, 0:128] = cosine
    out_ref[256:257, 128:256] = sine
    out_ref[257:258, 0:128] = -sine
    out_ref[257:258, 128:256] = cosine


def split(value):
    high = value.astype(jnp.bfloat16)
    rest = value - high.astype(jnp.float32)
    middle = rest.astype(jnp.bfloat16)
    low = (rest - middle.astype(jnp.float32)).astype(jnp.bfloat16)
    return high, middle, low


def product(factor, solved, lane):
    width = solved.shape[1]

    def placed(part):
        parts = [part]
        if lane:
            parts = [jnp.zeros((lane, width), jnp.bfloat16)] + parts
        if lane + CHUNK < 128:
            parts = parts + [jnp.zeros((128 - lane - CHUNK, width), jnp.bfloat16)]
        return jnp.concatenate(parts, axis=0)

    high, middle, low = split(factor)
    upper, centre, lower = [placed(part) for part in split(solved)]

    def multiplied(left, right):
        return jnp.dot(
            jnp.concatenate(left, axis=1),
            jnp.concatenate(right, axis=0),
            preferred_element_type=jnp.float32,
        )

    return (
        multiplied((high, low), (lower, upper))
        + multiplied((high, middle), (centre, centre))
        + multiplied((high, middle), (upper, upper))
    )


def array_kernel(start_ref, other_ref, out_ref, work_ref):
    other = flat_half(other_ref)
    work_ref[0:256, 0:256] = start_ref[0:256, 0:256] + square(other) / SNAPS
    work_ref[0:256, 256:384] = start_ref[0:256, 256:384] + own_columns(
        other, 1 - lax.axis_index("core")
    )
    work_ref[256:264, :] = start_ref[256:264, :]
    work_ref[264:272, :] = jnp.zeros((8, 384), jnp.float32)

    for base in range(0, 256, CHUNK):
        stop = base + CHUNK
        first = base // 128
        lane = base % 128
        groups = [0, 1, 2] if base < MOVE else [first, 1 - first]
        after = [g for g in groups if base < MOVE or g == 0 or stop < 256]
        near = min(stop + NEAR, ROWS) if stop < 256 else 264
        rows = [
            [work_ref[r : r + 8, 128 * g : 128 * g + 128] for g in groups]
            for r in range(base, stop, 8)
        ]
        spread = {
            r: [
                lanes_of(work_ref[r : r + 8, 128 * first : 128 * first + 128], lane + t)
                for t in range(CHUNK)
            ]
            for r in range(stop, near, 8)
        }
        rows = eliminate(rows, lane, CHUNK)
        rows = [[row[groups.index(g)] for g in after] for row in rows]
        for i, g in enumerate(after):
            lines = [row_of(rows[t // 8][i], t % 8) for t in range(CHUNK)]
            span = slice(128 * g, 128 * g + 128)
            for r in range(stop, near, 8):
                work_ref[r : r + 8, span] = less_product(work_ref[r : r + 8, span], spread[r], lines)
        if near < ROWS:
            factor = work_ref[near:ROWS, 128 * first : 128 * first + 128]
            solved = jnp.concatenate([jnp.concatenate(row, axis=1) for row in rows], axis=0)
            delta = product(factor, solved, lane)
            for i, g in enumerate(after):
                span = slice(128 * g, 128 * g + 128)
                work_ref[near:ROWS, span] = work_ref[near:ROWS, span] - delta[:, 128 * i : 128 * i + 128]
        if stop == MOVE:
            moved = lax.broadcasted_iota(jnp.int32, (8, 128), 1) < 18
            for r in range(stop, ROWS, 8):
                work_ref[r : r + 8, 0:128] = jnp.where(
                    moved, work_ref[r : r + 8, 256:384], work_ref[r : r + 8, 0:128]
                )

    final = -work_ref[256:264, 0:128]
    upper = row_of(final, 0)
    lower = row_of(final, 1)
    g00 = lanes_of(upper, 16)
    g01 = lanes_of(upper, 17)
    g10 = lanes_of(lower, 16)
    g11 = lanes_of(lower, 17)
    scale = math.sqrt(128.0) / (g00 * g11 - g01 * g10)
    first_row = (g11 * upper - g10 * lower) * scale
    second_row = (g00 * lower - g01 * upper) * scale
    place = lax.broadcasted_iota(jnp.int32, (8, 128), 0)
    out_ref[...] = jnp.where(place == 0, first_row, second_row)[0:2, 0:16]


def body(snapshots, beam_codes, panel_codes, loading):
    message = pl.pallas_call(
        message_kernel,
        out_shape=jax.ShapeDtypeStruct((16, 80, 128), jnp.bfloat16),
        in_specs=[vmem(), vmem()],
        out_specs=vmem(),
        compiler_params=limit(4),
        name="message",
    )(snapshots.reshape(8, 16, SNAPS), beam_codes.T)
    got = lax.all_to_all(message, ("tile_y", "tile_z"), 0, 0, tiled=True)
    beams = pl.pallas_call(
        beams_kernel,
        out_shape=jax.ShapeDtypeStruct((64, SNAPS), jnp.float32),
        in_specs=[vmem()],
        out_specs=vmem(),
        compiler_params=limit(4),
        name="beams",
    )(got)
    other = lax.ppermute(beams, "core", [(0, 1), (1, 0)])
    lines = pl.pallas_call(
        cancel_kernel,
        out_shape=jax.ShapeDtypeStruct((640, 128), jnp.float32),
        in_specs=[smem(), vmem(), vmem()],
        out_specs=vmem(),
        compiler_params=limit(4),
        name="cancel",
    )(loading, beams, other)
    lines = lines.reshape(128, 5, 1, 128)
    gathered = lax.all_to_all(lines, ("panel", "tile_y"), 0, 0, tiled=True)
    gathered = gathered.reshape(640, 128)
    other = lax.ppermute(gathered, "core", [(0, 1), (1, 0)])
    cancel, start = pl.pallas_call(
        own_kernel,
        out_shape=(
            jax.ShapeDtypeStruct((8, 2, 62), jnp.float32),
            jax.ShapeDtypeStruct((264, 384), jnp.float32),
        ),
        in_specs=[vmem(), vmem()],
        out_specs=(vmem(), vmem()),
        compiler_params=limit(8),
        cost_estimate=pl.CostEstimate(flops=400000000, bytes_accessed=800000, transcendentals=0),
        name="own",
    )(panel_codes.reshape(1, 128), gathered)
    beam_out = pl.pallas_call(
        array_kernel,
        out_shape=jax.ShapeDtypeStruct((2, 16), jnp.float32),
        in_specs=[vmem(), vmem()],
        out_specs=vmem(),
        scratch_shapes=[pltpu.VMEM((ROWS, 384), jnp.float32)],
        compiler_params=limit(8),
        name="array",
    )(start, other)
    return cancel.transpose(0, 2, 1), beam_out


def solution(mesh):
    torus = Mesh(
        mesh.devices.reshape(mesh.shape["panel"], 8, 2, 2), ("panel", "tile_y", "tile_z", "core")
    )
    return jax.shard_map(
        body,
        mesh=torus,
        in_specs=(P("panel", TILE, None, None), P(None, TILE), P(), P("panel")),
        out_specs=(P("panel", None, None), P(None, TILE)),
        check_vma=False,
    )
```

```python
import math

import jax
import jax.numpy as jnp
from jax import lax
from jax.experimental import pallas as pl
from jax.experimental.pallas import tpu as pltpu
from jax.sharding import Mesh
from jax.sharding import PartitionSpec as P

SNAPS = 512
PHASE_LEVELS = 64
ARRAY_LOAD = 1.0
TILE = ("tile_y", "tile_z", "core")
CHUNK = 16
NEAR = 16
MOVE = 32
ROWS = 272
HIGHEST = lax.Precision.HIGHEST


def vmem():
    return pl.BlockSpec(memory_space=pltpu.VMEM)


def limit(mebibytes):
    return pltpu.CompilerParams(vmem_limit_bytes=mebibytes << 20)


def lanes_of(block, lane):
    return jnp.broadcast_to(block[:, lane : lane + 1], (8, 128))


def row_of(block, row):
    return jnp.broadcast_to(block[row : row + 1, :], (8, 128))


def eliminate(rows, first_lane, steps):
    rows = [list(row) for row in rows]
    place = lax.broadcasted_iota(jnp.int32, (8, 128), 0)
    spread = [[lanes_of(row[0], first_lane + u) for u in range(steps)] for row in rows]
    same = [jnp.ones((8, 128), jnp.float32) for row in rows]
    twin = [jnp.zeros((8, 128), jnp.float32) for row in rows]
    for t in range(0, steps, 2):
        own, s = divmod(t, 8)
        a = row_of(spread[own][t], s)
        b = row_of(spread[own][t + 1], s)
        c = row_of(spread[own][t + 1], s + 1)
        scale = 1.0 / (a * c - b * b)
        raw = (a, b, c)
        a, b, c = a * scale, b * scale, c * scale
        pair = (place == s) | (place == s + 1)
        same[own] = jnp.where(place == s, c, jnp.where(place == s + 1, a, same[own]))
        twin[own] = jnp.where(pair, -b, twin[own])
        first = [c * row[t] - b * row[t + 1] for row in spread]
        second = [a * row[t + 1] - b * row[t] for row in spread]
        first[own] = jnp.where(pair, 0.0, first[own])
        second[own] = jnp.where(pair, 0.0, second[own])

        def reduce(blocks):
            upper = row_of(blocks[own], s)
            lower = row_of(blocks[own], s + 1)
            return [
                block - (f * upper + h * lower) for block, f, h in zip(blocks, first, second)
            ]

        for u in range(t + 2, steps):
            quick = None
            if u < t + 4:
                target = (t + 2) // 8
                upper = row_of(spread[own][u], s)
                lower = row_of(spread[own][u], s + 1)
                block = spread[target]
                f = raw[2] * block[t] - raw[1] * block[t + 1]
                h = raw[0] * block[t + 1] - raw[1] * block[t]
                change = f * upper + h * lower
                if target == own:
                    change = jnp.where(pair, 0.0, change)
                quick = block[u] - change * scale
            for row, value in zip(spread, reduce([row[u] for row in spread])):
                row[u] = value
            if quick is not None:
                spread[target][u] = quick
        for g in range(len(rows[0])):
            for row, value in zip(rows, reduce([row[g] for row in rows])):
                row[g] = value

    def scaled(value, i):
        lines = [row_of(value, s ^ 1) for s in range(8)]
        for step in (1, 2, 4):
            lines = [
                jnp.where((place & step) == 0, lines[2 * j], lines[2 * j + 1])
                for j in range(len(lines) // 2)
            ]
        swapped = lines[0]
        return value * same[i] + swapped * twin[i]

    return [[scaled(value, i) for value in row] for i, row in enumerate(rows)]


def less_product(value, spread, lines):
    terms = [f * line for f, line in zip(spread, lines)]
    while len(terms) > 1:
        terms = [sum(terms[i : i + 2]) for i in range(0, len(terms), 2)]
    return value - terms[0]


def forward(rows, steps):
    rows = [list(row) for row in rows]
    for first in range(0, steps, CHUNK):
        count = min(CHUNK, steps - first)
        own = range(first // 8, (first + count + 7) // 8)
        below = range(own.stop, len(rows))
        spread = {i: [lanes_of(rows[i][0], first + t) for t in range(count)] for i in below}
        solved = eliminate([rows[i] for i in own], first, count)
        for i, row in zip(own, solved):
            rows[i] = row
        for g in range(len(rows[0])):
            lines = [row_of(solved[t // 8][g], t % 8) for t in range(count)]
            for i in below:
                rows[i][g] = less_product(rows[i][g], spread[i], lines)
    return rows


def cosine_of(steps):
    quarter = (steps + 8) >> 4
    angle = (steps - 16 * quarter).astype(jnp.float32) * (2.0 * math.pi / PHASE_LEVELS)
    square = angle * angle
    cosine = 1.0 + square * (
        -1 / 2 + square * (1 / 24 + square * (-1 / 720 + square * (1 / 40320 - square / 3628800)))
    )
    sine = angle * (
        1.0 + square * (-1 / 6 + square * (1 / 120 + square * (-1 / 5040 + square / 362880)))
    )
    value = jnp.where((quarter & 1) == 0, cosine, sine)
    return jnp.where(((quarter + 1) & 2) == 0, value, -value)


def message_kernel(samples_ref, codes_ref, panel_codes_ref, loading_ref, out_ref, side_ref):
    side_ref[0:1, :] = cosine_of(panel_codes_ref[...])
    side_ref[1:2, :] = cosine_of(panel_codes_ref[...] - 16)
    own = lax.broadcasted_iota(jnp.int32, (1, 8), 1) == lax.axis_index("tile_y")
    load = jnp.sum(jnp.where(own, loading_ref[...], 0.0), axis=1, keepdims=True)
    side_ref[2:8, :] = jnp.broadcast_to(load, (6, 128))
    codes = jnp.concatenate([codes_ref[...], jnp.zeros((8, 96), jnp.int32)], axis=1)
    row = lax.broadcasted_iota(jnp.int32, (8, 128), 0)
    lane = lax.broadcasted_iota(jnp.int32, (8, 128), 1)
    real = pltpu.roll(codes, 127, 1)
    imag = pltpu.roll(codes, 30, 1)
    last = pltpu.roll(codes, 62, 1)
    twin = pltpu.roll(codes, 63, 1)
    codes = jnp.where(lane < 31, real, jnp.where(lane < 62, imag, last))
    codes = jnp.where(lane == 63, twin, codes)
    imaginary = jnp.where((lane >= 31) & (lane != 62), 1, 0)

    def columns(first):
        spread = row_of(codes, first)
        for t in range(1, 4):
            spread = jnp.where(row >= 2 * t, row_of(codes, first + t), spread)
        return cosine_of(spread + 16 * (imaginary - (row & 1)))

    table = jnp.concatenate([columns(0), columns(4)], axis=0)
    table = (table / math.sqrt(256)).astype(jnp.bfloat16)
    for p in range(8):
        for z in range(2):
            for b in range(4):
                out_ref[2 * p + z, 16 * b : 16 * b + 16, :] = samples_ref[
                    p, :, 128 * b : 128 * b + 128
                ]
            out_ref[2 * p + z, 64:80, :] = table


def beams_kernel(got_ref, beams_ref):
    got = got_ref[...]
    table = got[:, 64:80, :].reshape(256, 128)
    samples = jnp.concatenate(
        [got[:, 16 * b : 16 * b + 16, :].reshape(256, 128) for b in range(4)], axis=1
    )
    beams_ref[...] = lax.dot_general(
        table, samples, (((0,), (0,)), ((), ())), preferred_element_type=jnp.float32
    )[:64]


def cancel_kernel(side_ref, beams_ref, out_ref):
    load = side_ref[2:3, 0:64]
    core = lax.axis_index("core")
    beams = beams_ref[0] + beams_ref[1]
    covar = square(beams) / SNAPS
    row = lax.broadcasted_iota(jnp.int32, (64, 64), 0)
    column = lax.broadcasted_iota(jnp.int32, (64, 64), 1)
    covar = covar + jnp.where(row == column, jnp.broadcast_to(load, (64, 64)), 0.0)
    covar = jnp.concatenate([covar, jnp.zeros((64, 64), jnp.float32)], axis=1)
    half = jnp.where(core == 0, beams[:, :256], beams[:, 256:])
    row = lax.broadcasted_iota(jnp.int32, (64, 128), 0)
    column = lax.broadcasted_iota(jnp.int32, (64, 128), 1) & 63
    source = jnp.where(column < 62, column // 2 + 31 * (column & 1), 64)
    identity = jnp.where(row == source, 1.0, 0.0)
    whole = jnp.concatenate([covar, half, identity], axis=1)
    rows = [
        [whole[8 * i : 8 * i + 8, 128 * g : 128 * g + 128] for g in range(4)] for i in range(8)
    ]
    last = forward(rows, 62)[7]
    lane = lax.broadcasted_iota(jnp.int32, (1, 128), 1)
    cancel = jnp.where(lane < 64, -last[3][6:7, :], -last[3][7:8, :])
    line = jnp.concatenate([last[1][6:8, :], last[2][6:8, :], cancel], axis=0)
    for i in range(8):
        out_ref[5 * i : 5 * i + 5, :] = line
    lines = out_ref[0:40, :]
    for i in range(1, 16):
        out_ref[40 * i : 40 * i + 40, :] = lines


def square(value):
    return lax.dot_general(
        value,
        value,
        (((1,), (1,)), ((), ())),
        precision=HIGHEST,
        preferred_element_type=jnp.float32,
    )


def split(value):
    high = value.astype(jnp.bfloat16)
    rest = value - high.astype(jnp.float32)
    middle = rest.astype(jnp.bfloat16)
    low = (rest - middle.astype(jnp.float32)).astype(jnp.bfloat16)
    return high, middle, low


def product(factor, solved, lane):
    width = solved.shape[1]

    def placed(part):
        parts = [part]
        if lane:
            parts = [jnp.zeros((lane, width), jnp.bfloat16)] + parts
        if lane + CHUNK < 128:
            parts = parts + [jnp.zeros((128 - lane - CHUNK, width), jnp.bfloat16)]
        return jnp.concatenate(parts, axis=0)

    high, middle, low = split(factor)
    upper, centre, lower = [placed(part) for part in split(solved)]

    def multiplied(left, right):
        return jnp.dot(
            jnp.concatenate(left, axis=1),
            jnp.concatenate(right, axis=0),
            preferred_element_type=jnp.float32,
        )

    return (
        multiplied((high, low), (lower, upper))
        + multiplied((high, middle), (centre, centre))
        + multiplied((high, middle), (upper, upper))
    )


def array_kernel(side_ref, lines_ref, cancel_ref, out_ref, work_ref):
    y = lax.axis_index("tile_y")
    cancel = lines_ref[pl.ds(lax.axis_index("panel") * 40 + 4, 8, stride=5), :]
    cancel_ref[:, 0, :] = cancel[:, :62]
    cancel_ref[:, 1, :] = pltpu.roll(cancel, 64, 1)[:, :62]

    blocks = [
        [lines_ref[pl.ds(640 * h + 2 * b + k, 128, stride=5), :] for h in range(2) for b in range(2)]
        for k in range(2)
    ]
    flat = jnp.concatenate([jnp.concatenate(row, axis=1) for row in blocks], axis=0)
    row = lax.broadcasted_iota(jnp.int32, (256, 256), 0)
    column = lax.broadcasted_iota(jnp.int32, (256, 256), 1)
    work_ref[0:256, 0:256] = square(flat) / SNAPS + jnp.where(row == column, ARRAY_LOAD, 0.0)

    cosine = side_ref[0:1, :]
    sine = side_ref[1:2, :]
    spread_cosine = jnp.broadcast_to(cosine, (128, 128)).T
    spread_sine = jnp.broadcast_to(sine, (128, 128)).T
    block = y // 2
    slot = (y % 2) * 4 + lax.axis_index("tile_z") * 2 + lax.axis_index("core")
    mine = jnp.where(
        block < 2,
        jnp.where(block == 0, flat[:, 0:128], flat[:, 128:256]),
        jnp.where(block == 2, flat[:, 256:384], flat[:, 384:512]),
    )
    mine = pltpu.roll(mine, lax.rem(128 - 16 * slot, 128), 1)
    lane = lax.broadcasted_iota(jnp.int32, (128, 128), 1)

    def right_side(values, first, second):
        values = jnp.where(lane < 16, values, 0.0)
        return jnp.where(lane == 16, first, jnp.where(lane == 17, second, values))

    work_ref[0:128, 256:384] = right_side(mine[:128], spread_cosine, -spread_sine)
    work_ref[128:256, 256:384] = right_side(mine[128:], spread_sine, spread_cosine)
    work_ref[256:ROWS, :] = jnp.zeros((ROWS - 256, 384), jnp.float32)
    work_ref[256:257, 0:128] = cosine
    work_ref[256:257, 128:256] = sine
    work_ref[257:258, 0:128] = -sine
    work_ref[257:258, 128:256] = cosine

    for base in range(0, 256, CHUNK):
        stop = base + CHUNK
        first = base // 128
        lane = base % 128
        groups = [0, 1, 2] if base < MOVE else [first, 1 - first]
        after = [g for g in groups if base < MOVE or g == 0 or stop < 256]
        near = min(stop + NEAR, ROWS) if stop < 256 else 264
        rows = [
            [work_ref[r : r + 8, 128 * g : 128 * g + 128] for g in groups]
            for r in range(base, stop, 8)
        ]
        spread = {
            r: [
                lanes_of(work_ref[r : r + 8, 128 * first : 128 * first + 128], lane + t)
                for t in range(CHUNK)
            ]
            for r in range(stop, near, 8)
        }
        rows = eliminate(rows, lane, CHUNK)
        rows = [[row[groups.index(g)] for g in after] for row in rows]
        for i, g in enumerate(after):
            lines = [row_of(rows[t // 8][i], t % 8) for t in range(CHUNK)]
            span = slice(128 * g, 128 * g + 128)
            for r in range(stop, near, 8):
                work_ref[r : r + 8, span] = less_product(work_ref[r : r + 8, span], spread[r], lines)
        if near < ROWS:
            factor = work_ref[near:ROWS, 128 * first : 128 * first + 128]
            solved = jnp.concatenate([jnp.concatenate(row, axis=1) for row in rows], axis=0)
            delta = product(factor, solved, lane)
            for i, g in enumerate(after):
                span = slice(128 * g, 128 * g + 128)
                work_ref[near:ROWS, span] = work_ref[near:ROWS, span] - delta[:, 128 * i : 128 * i + 128]
        if stop == MOVE:
            moved = lax.broadcasted_iota(jnp.int32, (8, 128), 1) < 18
            for r in range(stop, ROWS, 8):
                work_ref[r : r + 8, 0:128] = jnp.where(
                    moved, work_ref[r : r + 8, 256:384], work_ref[r : r + 8, 0:128]
                )

    final = -work_ref[256:264, 0:128]
    upper = row_of(final, 0)
    lower = row_of(final, 1)
    g00 = lanes_of(upper, 16)
    g01 = lanes_of(upper, 17)
    g10 = lanes_of(lower, 16)
    g11 = lanes_of(lower, 17)
    scale = math.sqrt(128.0) / (g00 * g11 - g01 * g10)
    first_row = (g11 * upper - g10 * lower) * scale
    second_row = (g00 * lower - g01 * upper) * scale
    place = lax.broadcasted_iota(jnp.int32, (8, 128), 0)
    out_ref[...] = jnp.where(place == 0, first_row, second_row)[0:2, 0:16]


def body(snapshots, beam_codes, panel_codes, loading):
    message, side = pl.pallas_call(
        message_kernel,
        out_shape=(
            jax.ShapeDtypeStruct((16, 80, 128), jnp.bfloat16),
            jax.ShapeDtypeStruct((8, 128), jnp.float32),
        ),
        in_specs=[vmem()] * 4,
        out_specs=(vmem(), vmem()),
        compiler_params=limit(4),
        name="message",
    )(
        snapshots.reshape(8, 16, SNAPS),
        beam_codes.T,
        panel_codes.reshape(1, 128),
        loading.reshape(1, 8),
    )
    got = lax.all_to_all(message, ("tile_y", "tile_z"), 0, 0, tiled=True)
    beams = pl.pallas_call(
        beams_kernel,
        out_shape=jax.ShapeDtypeStruct((64, SNAPS), jnp.float32),
        in_specs=[vmem()],
        out_specs=vmem(),
        compiler_params=limit(4),
        name="beams",
    )(got)
    beams = lax.all_gather(beams, "core")
    lines = pl.pallas_call(
        cancel_kernel,
        out_shape=jax.ShapeDtypeStruct((640, 128), jnp.float32),
        in_specs=[vmem(), vmem()],
        out_specs=vmem(),
        compiler_params=limit(4),
        name="cancel",
    )(side, beams)
    lines = lines.reshape(128, 5, 1, 128)
    gathered = lax.all_to_all(lines, ("panel", "tile_y"), 0, 0, tiled=True)
    gathered = lax.all_gather(gathered.reshape(640, 128), "core", tiled=True)
    cancel, beam_out = pl.pallas_call(
        array_kernel,
        out_shape=(
            jax.ShapeDtypeStruct((8, 2, 62), jnp.float32),
            jax.ShapeDtypeStruct((2, 16), jnp.float32),
        ),
        in_specs=[vmem(), vmem()],
        out_specs=(vmem(), vmem()),
        scratch_shapes=[pltpu.VMEM((ROWS, 384), jnp.float32)],
        compiler_params=limit(8),
        name="array",
    )(side, gathered)
    return cancel.transpose(0, 2, 1), beam_out


def solution(mesh):
    torus = Mesh(
        mesh.devices.reshape(mesh.shape["panel"], 8, 2, 2), ("panel", "tile_y", "tile_z", "core")
    )
    return jax.shard_map(
        body,
        mesh=torus,
        in_specs=(P("panel", TILE, None, None), P(None, TILE), P(), P("panel")),
        out_specs=(P("panel", None, None), P(None, TILE)),
        check_vma=False,
    )
```

```python
import math

import jax
import jax.numpy as jnp
from jax import lax
from jax.experimental import pallas as pl
from jax.experimental.pallas import tpu as pltpu
from jax.sharding import Mesh
from jax.sharding import PartitionSpec as P

SNAPS = 512
PHASE_LEVELS = 64
ARRAY_LOAD = 1.0
TILE = ("tile_y", "tile_z", "core")
CHUNK = 16
NEAR = 16
MOVE = 32
ROWS = 272
HIGHEST = lax.Precision.HIGHEST


def vmem():
    return pl.BlockSpec(memory_space=pltpu.VMEM)


def limit(mebibytes):
    return pltpu.CompilerParams(vmem_limit_bytes=mebibytes << 20)


def lanes_of(block, lane):
    return jnp.broadcast_to(block[:, lane : lane + 1], (8, 128))


def row_of(block, row):
    return jnp.broadcast_to(block[row : row + 1, :], (8, 128))


def eliminate(rows, first_lane, steps):
    rows = [list(row) for row in rows]
    place = lax.broadcasted_iota(jnp.int32, (8, 128), 0)
    spread = [[lanes_of(row[0], first_lane + u) for u in range(steps)] for row in rows]
    same = [jnp.ones((8, 128), jnp.float32) for row in rows]
    twin = [jnp.zeros((8, 128), jnp.float32) for row in rows]
    for t in range(0, steps, 2):
        own, s = divmod(t, 8)
        a = row_of(spread[own][t], s)
        b = row_of(spread[own][t + 1], s)
        c = row_of(spread[own][t + 1], s + 1)
        scale = 1.0 / (a * c - b * b)
        raw = (a, b, c)
        a, b, c = a * scale, b * scale, c * scale
        pair = (place == s) | (place == s + 1)
        same[own] = jnp.where(place == s, c, jnp.where(place == s + 1, a, same[own]))
        twin[own] = jnp.where(pair, -b, twin[own])
        first = [c * row[t] - b * row[t + 1] for row in spread]
        second = [a * row[t + 1] - b * row[t] for row in spread]
        first[own] = jnp.where(pair, 0.0, first[own])
        second[own] = jnp.where(pair, 0.0, second[own])

        def reduce(blocks):
            upper = row_of(blocks[own], s)
            lower = row_of(blocks[own], s + 1)
            return [
                block - (f * upper + h * lower) for block, f, h in zip(blocks, first, second)
            ]

        for u in range(t + 2, steps):
            quick = None
            if u < t + 4:
                target = (t + 2) // 8
                upper = row_of(spread[own][u], s)
                lower = row_of(spread[own][u], s + 1)
                block = spread[target]
                f = raw[2] * block[t] - raw[1] * block[t + 1]
                h = raw[0] * block[t + 1] - raw[1] * block[t]
                change = f * upper + h * lower
                if target == own:
                    change = jnp.where(pair, 0.0, change)
                quick = block[u] - change * scale
            for row, value in zip(spread, reduce([row[u] for row in spread])):
                row[u] = value
            if quick is not None:
                spread[target][u] = quick
        for g in range(len(rows[0])):
            for row, value in zip(rows, reduce([row[g] for row in rows])):
                row[g] = value

    def scaled(value, i):
        lines = [row_of(value, s ^ 1) for s in range(8)]
        for step in (1, 2, 4):
            lines = [
                jnp.where((place & step) == 0, lines[2 * j], lines[2 * j + 1])
                for j in range(len(lines) // 2)
            ]
        swapped = lines[0]
        return value * same[i] + swapped * twin[i]

    return [[scaled(value, i) for value in row] for i, row in enumerate(rows)]


def less_product(value, spread, lines):
    terms = [f * line for f, line in zip(spread, lines)]
    while len(terms) > 1:
        terms = [sum(terms[i : i + 2]) for i in range(0, len(terms), 2)]
    return value - terms[0]


def forward(rows, steps):
    rows = [list(row) for row in rows]
    for first in range(0, steps, CHUNK):
        count = min(CHUNK, steps - first)
        own = range(first // 8, (first + count + 7) // 8)
        below = range(own.stop, len(rows))
        spread = {i: [lanes_of(rows[i][0], first + t) for t in range(count)] for i in below}
        solved = eliminate([rows[i] for i in own], first, count)
        for i, row in zip(own, solved):
            rows[i] = row
        for g in range(len(rows[0])):
            lines = [row_of(solved[t // 8][g], t % 8) for t in range(count)]
            for i in below:
                rows[i][g] = less_product(rows[i][g], spread[i], lines)
    return rows


def cosine_of(steps):
    quarter = (steps + 8) >> 4
    angle = (steps - 16 * quarter).astype(jnp.float32) * (2.0 * math.pi / PHASE_LEVELS)
    square = angle * angle
    cosine = 1.0 + square * (
        -1 / 2 + square * (1 / 24 + square * (-1 / 720 + square * (1 / 40320 - square / 3628800)))
    )
    sine = angle * (
        1.0 + square * (-1 / 6 + square * (1 / 120 + square * (-1 / 5040 + square / 362880)))
    )
    value = jnp.where((quarter & 1) == 0, cosine, sine)
    return jnp.where(((quarter + 1) & 2) == 0, value, -value)


def identity_kernel(out_ref):
    row = lax.broadcasted_iota(jnp.int32, (64, 128), 0)
    column = lax.broadcasted_iota(jnp.int32, (64, 128), 1) & 63
    source = jnp.where(column < 62, column // 2 + 31 * (column & 1), 64)
    out_ref[...] = jnp.where(row == source, 1.0, 0.0)


def message_kernel(_, samples_ref, codes_ref, panel_codes_ref, loading_ref, out_ref, side_ref):
    side_ref[0:1, :] = cosine_of(panel_codes_ref[...])
    side_ref[1:2, :] = cosine_of(panel_codes_ref[...] - 16)
    own = lax.broadcasted_iota(jnp.int32, (1, 8), 1) == lax.axis_index("tile_y")
    load = jnp.sum(jnp.where(own, loading_ref[...], 0.0), axis=1, keepdims=True)
    side_ref[2:8, :] = jnp.broadcast_to(load, (6, 128))
    codes = jnp.concatenate([codes_ref[...], jnp.zeros((8, 96), jnp.int32)], axis=1)
    row = lax.broadcasted_iota(jnp.int32, (8, 128), 0)
    lane = lax.broadcasted_iota(jnp.int32, (8, 128), 1)
    real = pltpu.roll(codes, 127, 1)
    imag = pltpu.roll(codes, 30, 1)
    last = pltpu.roll(codes, 62, 1)
    twin = pltpu.roll(codes, 63, 1)
    codes = jnp.where(lane < 31, real, jnp.where(lane < 62, imag, last))
    codes = jnp.where(lane == 63, twin, codes)
    imaginary = jnp.where((lane >= 31) & (lane != 62), 1, 0)

    def columns(first):
        spread = row_of(codes, first)
        for t in range(1, 4):
            spread = jnp.where(row >= 2 * t, row_of(codes, first + t), spread)
        return cosine_of(spread + 16 * (imaginary - (row & 1)))

    table = jnp.concatenate([columns(0), columns(4)], axis=0)
    table = (table / math.sqrt(256)).astype(jnp.bfloat16)
    for p in range(8):
        samples = samples_ref[p].reshape(16, SNAPS)
        for z in range(2):
            for b in range(4):
                out_ref[2 * p + z, 16 * b : 16 * b + 16, :] = samples[:, 128 * b : 128 * b + 128]
            out_ref[2 * p + z, 64:80, :] = table


def beams_kernel(got_ref, beams_ref):
    got = got_ref[...]
    table = got[:, 64:80, :].reshape(256, 128)
    samples = jnp.concatenate(
        [got[:, 16 * b : 16 * b + 16, :].reshape(256, 128) for b in range(4)], axis=1
    )
    beams_ref[...] = lax.dot_general(
        table, samples, (((0,), (0,)), ((), ())), preferred_element_type=jnp.float32
    )[:64]


def cancel_kernel(side_ref, identity_ref, beams_ref, out_ref):
    load = side_ref[2:3, 0:64]
    core = lax.axis_index("core")
    beams = beams_ref[0] + beams_ref[1]
    covar = square(beams) / SNAPS
    row = lax.broadcasted_iota(jnp.int32, (64, 64), 0)
    column = lax.broadcasted_iota(jnp.int32, (64, 64), 1)
    covar = covar + jnp.where(row == column, jnp.broadcast_to(load, (64, 64)), 0.0)
    covar = jnp.concatenate([covar, jnp.zeros((64, 64), jnp.float32)], axis=1)
    half = jnp.where(core == 0, beams[:, :256], beams[:, 256:])
    whole = jnp.concatenate([covar, half, identity_ref[...]], axis=1)
    rows = [
        [whole[8 * i : 8 * i + 8, 128 * g : 128 * g + 128] for g in range(4)] for i in range(8)
    ]
    last = forward(rows, 62)[7]
    lane = lax.broadcasted_iota(jnp.int32, (1, 128), 1)
    cancel = jnp.where(lane < 64, -last[3][6:7, :], -last[3][7:8, :])
    line = jnp.concatenate([last[1][6:8, :], last[2][6:8, :], cancel], axis=0)
    for i in range(8):
        out_ref[5 * i : 5 * i + 5, :] = line
    lines = out_ref[0:40, :]
    for i in range(1, 16):
        out_ref[40 * i : 40 * i + 40, :] = lines


def square(value):
    return lax.dot_general(
        value,
        value,
        (((1,), (1,)), ((), ())),
        precision=HIGHEST,
        preferred_element_type=jnp.float32,
    )


def split(value):
    high = value.astype(jnp.bfloat16)
    rest = value - high.astype(jnp.float32)
    middle = rest.astype(jnp.bfloat16)
    low = (rest - middle.astype(jnp.float32)).astype(jnp.bfloat16)
    return high, middle, low


def product(factor, solved, lane):
    width = solved.shape[1]

    def placed(part):
        parts = [part]
        if lane:
            parts = [jnp.zeros((lane, width), jnp.bfloat16)] + parts
        if lane + CHUNK < 128:
            parts = parts + [jnp.zeros((128 - lane - CHUNK, width), jnp.bfloat16)]
        return jnp.concatenate(parts, axis=0)

    high, middle, low = split(factor)
    upper, centre, lower = [placed(part) for part in split(solved)]

    def multiplied(left, right):
        return jnp.dot(
            jnp.concatenate(left, axis=1),
            jnp.concatenate(right, axis=0),
            preferred_element_type=jnp.float32,
        )

    return (
        multiplied((high, low), (lower, upper))
        + multiplied((high, middle), (centre, centre))
        + multiplied((high, middle), (upper, upper))
    )


def array_kernel(side_ref, lines_ref, cancel_ref, out_ref, work_ref):
    y = lax.axis_index("tile_y")
    cancel = lines_ref[pl.ds(lax.axis_index("panel") * 40 + 4, 8, stride=5), :]
    cancel_ref[:, 0, :] = cancel[:, :62]
    cancel_ref[:, 1, :] = pltpu.roll(cancel, 64, 1)[:, :62]

    blocks = [
        [lines_ref[pl.ds(640 * h + 2 * b + k, 128, stride=5), :] for h in range(2) for b in range(2)]
        for k in range(2)
    ]
    flat = jnp.concatenate([jnp.concatenate(row, axis=1) for row in blocks], axis=0)
    row = lax.broadcasted_iota(jnp.int32, (256, 256), 0)
    column = lax.broadcasted_iota(jnp.int32, (256, 256), 1)
    work_ref[0:256, 0:256] = square(flat) / SNAPS + jnp.where(row == column, ARRAY_LOAD, 0.0)

    cosine = side_ref[0:1, :]
    sine = side_ref[1:2, :]
    spread_cosine = jnp.broadcast_to(cosine, (128, 128)).T
    spread_sine = jnp.broadcast_to(sine, (128, 128)).T
    block = y // 2
    slot = (y % 2) * 4 + lax.axis_index("tile_z") * 2 + lax.axis_index("core")
    mine = jnp.where(
        block < 2,
        jnp.where(block == 0, flat[:, 0:128], flat[:, 128:256]),
        jnp.where(block == 2, flat[:, 256:384], flat[:, 384:512]),
    )
    mine = pltpu.roll(mine, lax.rem(128 - 16 * slot, 128), 1)
    lane = lax.broadcasted_iota(jnp.int32, (128, 128), 1)

    def right_side(values, first, second):
        values = jnp.where(lane < 16, values, 0.0)
        return jnp.where(lane == 16, first, jnp.where(lane == 17, second, values))

    work_ref[0:128, 256:384] = right_side(mine[:128], spread_cosine, -spread_sine)
    work_ref[128:256, 256:384] = right_side(mine[128:], spread_sine, spread_cosine)
    work_ref[256:ROWS, :] = jnp.zeros((ROWS - 256, 384), jnp.float32)
    work_ref[256:257, 0:128] = cosine
    work_ref[256:257, 128:256] = sine
    work_ref[257:258, 0:128] = -sine
    work_ref[257:258, 128:256] = cosine

    for base in range(0, 256, CHUNK):
        stop = base + CHUNK
        first = base // 128
        lane = base % 128
        groups = [0, 1, 2] if base < MOVE else [first, 1 - first]
        after = [g for g in groups if base < MOVE or g == 0 or stop < 256]
        near = min(stop + NEAR, ROWS) if stop < 256 else 264
        rows = [
            [work_ref[r : r + 8, 128 * g : 128 * g + 128] for g in groups]
            for r in range(base, stop, 8)
        ]
        spread = {
            r: [
                lanes_of(work_ref[r : r + 8, 128 * first : 128 * first + 128], lane + t)
                for t in range(CHUNK)
            ]
            for r in range(stop, near, 8)
        }
        rows = eliminate(rows, lane, CHUNK)
        rows = [[row[groups.index(g)] for g in after] for row in rows]
        for i, g in enumerate(after):
            lines = [row_of(rows[t // 8][i], t % 8) for t in range(CHUNK)]
            span = slice(128 * g, 128 * g + 128)
            for r in range(stop, near, 8):
                work_ref[r : r + 8, span] = less_product(work_ref[r : r + 8, span], spread[r], lines)
        if near < ROWS:
            factor = work_ref[near:ROWS, 128 * first : 128 * first + 128]
            solved = jnp.concatenate([jnp.concatenate(row, axis=1) for row in rows], axis=0)
            delta = product(factor, solved, lane)
            for i, g in enumerate(after):
                span = slice(128 * g, 128 * g + 128)
                work_ref[near:ROWS, span] = work_ref[near:ROWS, span] - delta[:, 128 * i : 128 * i + 128]
        if stop == MOVE:
            moved = lax.broadcasted_iota(jnp.int32, (8, 128), 1) < 18
            for r in range(stop, ROWS, 8):
                work_ref[r : r + 8, 0:128] = jnp.where(
                    moved, work_ref[r : r + 8, 256:384], work_ref[r : r + 8, 0:128]
                )

    final = -work_ref[256:264, 0:128]
    upper = row_of(final, 0)
    lower = row_of(final, 1)
    g00 = lanes_of(upper, 16)
    g01 = lanes_of(upper, 17)
    g10 = lanes_of(lower, 16)
    g11 = lanes_of(lower, 17)
    scale = math.sqrt(128.0) / (g00 * g11 - g01 * g10)
    first_row = (g11 * upper - g10 * lower) * scale
    second_row = (g00 * lower - g01 * upper) * scale
    place = lax.broadcasted_iota(jnp.int32, (8, 128), 0)
    out_ref[...] = jnp.where(place == 0, first_row, second_row)[0:2, 0:16]


def body(snapshots, beam_codes, panel_codes, loading):
    identity = pl.pallas_call(
        identity_kernel,
        out_shape=jax.ShapeDtypeStruct((64, 128), jnp.float32),
        out_specs=vmem(),
        compiler_params=limit(4),
        cost_estimate=pl.CostEstimate(
            flops=2000000000, bytes_accessed=4000000, transcendentals=0
        ),
        name="identity",
    )()
    message, side = pl.pallas_call(
        message_kernel,
        out_shape=(
            jax.ShapeDtypeStruct((16, 80, 128), jnp.bfloat16),
            jax.ShapeDtypeStruct((8, 128), jnp.float32),
        ),
        in_specs=[vmem()] * 5,
        out_specs=(vmem(), vmem()),
        compiler_params=limit(4),
        name="message",
    )(
        identity,
        snapshots,
        beam_codes.T,
        panel_codes.reshape(1, 128),
        loading.reshape(1, 8),
    )
    got = lax.all_to_all(message, ("tile_y", "tile_z"), 0, 0, tiled=True)
    beams = pl.pallas_call(
        beams_kernel,
        out_shape=jax.ShapeDtypeStruct((64, SNAPS), jnp.float32),
        in_specs=[vmem()],
        out_specs=vmem(),
        compiler_params=limit(4),
        name="beams",
    )(got)
    beams = lax.all_gather(beams, "core")
    lines = pl.pallas_call(
        cancel_kernel,
        out_shape=jax.ShapeDtypeStruct((640, 128), jnp.float32),
        in_specs=[vmem(), vmem(), vmem()],
        out_specs=vmem(),
        compiler_params=limit(4),
        name="cancel",
    )(side, identity, beams)
    lines = lines.reshape(128, 5, 1, 128)
    gathered = lax.all_to_all(lines, ("panel", "tile_y"), 0, 0, tiled=True)
    gathered = lax.all_gather(gathered.reshape(640, 128), "core", tiled=True)
    cancel, beam_out = pl.pallas_call(
        array_kernel,
        out_shape=(
            jax.ShapeDtypeStruct((8, 2, 62), jnp.float32),
            jax.ShapeDtypeStruct((2, 16), jnp.float32),
        ),
        in_specs=[vmem(), vmem()],
        out_specs=(vmem(), vmem()),
        scratch_shapes=[pltpu.VMEM((ROWS, 384), jnp.float32)],
        compiler_params=limit(8),
        name="array",
    )(side, gathered)
    return cancel.transpose(0, 2, 1), beam_out


def solution(mesh):
    torus = Mesh(
        mesh.devices.reshape(mesh.shape["panel"], 8, 2, 2), ("panel", "tile_y", "tile_z", "core")
    )
    return jax.shard_map(
        body,
        mesh=torus,
        in_specs=(P("panel", TILE, None, None), P(None, TILE), P(), P("panel")),
        out_specs=(P("panel", None, None), P(None, TILE)),
        check_vma=False,
    )
```

```python
import math

import jax
import jax.numpy as jnp
from jax import lax
from jax.experimental import pallas as pl
from jax.experimental.pallas import tpu as pltpu
from jax.sharding import Mesh
from jax.sharding import PartitionSpec as P

SNAPS = 512
PHASE_LEVELS = 64
ARRAY_LOAD = 1.0
TILE = ("tile_y", "tile_z", "core")
CHUNK = 16
NEAR = 16
MOVE = 32
ROWS = 272
HIGHEST = lax.Precision.HIGHEST


def vmem():
    return pl.BlockSpec(memory_space=pltpu.VMEM)


def limit(mebibytes):
    return pltpu.CompilerParams(vmem_limit_bytes=mebibytes << 20)


def lanes_of(block, lane):
    return jnp.broadcast_to(block[:, lane : lane + 1], (8, 128))


def row_of(block, row):
    return jnp.broadcast_to(block[row : row + 1, :], (8, 128))


def eliminate(rows, first_lane, steps):
    rows = [list(row) for row in rows]
    place = lax.broadcasted_iota(jnp.int32, (8, 128), 0)
    spread = [[lanes_of(row[0], first_lane + u) for u in range(steps)] for row in rows]
    same = [jnp.ones((8, 128), jnp.float32) for row in rows]
    twin = [jnp.zeros((8, 128), jnp.float32) for row in rows]
    for t in range(0, steps, 2):
        own, s = divmod(t, 8)
        a = row_of(spread[own][t], s)
        b = row_of(spread[own][t + 1], s)
        c = row_of(spread[own][t + 1], s + 1)
        scale = 1.0 / (a * c - b * b)
        raw = (a, b, c)
        a, b, c = a * scale, b * scale, c * scale
        pair = (place == s) | (place == s + 1)
        same[own] = jnp.where(place == s, c, jnp.where(place == s + 1, a, same[own]))
        twin[own] = jnp.where(pair, -b, twin[own])
        first = [c * row[t] - b * row[t + 1] for row in spread]
        second = [a * row[t + 1] - b * row[t] for row in spread]
        first[own] = jnp.where(pair, 0.0, first[own])
        second[own] = jnp.where(pair, 0.0, second[own])

        def reduce(blocks):
            upper = row_of(blocks[own], s)
            lower = row_of(blocks[own], s + 1)
            return [
                block - (f * upper + h * lower) for block, f, h in zip(blocks, first, second)
            ]

        for u in range(t + 2, steps):
            quick = None
            if u < t + 4:
                target = (t + 2) // 8
                upper = row_of(spread[own][u], s)
                lower = row_of(spread[own][u], s + 1)
                block = spread[target]
                f = raw[2] * block[t] - raw[1] * block[t + 1]
                h = raw[0] * block[t + 1] - raw[1] * block[t]
                change = f * upper + h * lower
                if target == own:
                    change = jnp.where(pair, 0.0, change)
                quick = block[u] - change * scale
            for row, value in zip(spread, reduce([row[u] for row in spread])):
                row[u] = value
            if quick is not None:
                spread[target][u] = quick
        for g in range(len(rows[0])):
            for row, value in zip(rows, reduce([row[g] for row in rows])):
                row[g] = value

    def scaled(value, i):
        lines = [row_of(value, s ^ 1) for s in range(8)]
        for step in (1, 2, 4):
            lines = [
                jnp.where((place & step) == 0, lines[2 * j], lines[2 * j + 1])
                for j in range(len(lines) // 2)
            ]
        swapped = lines[0]
        return value * same[i] + swapped * twin[i]

    return [[scaled(value, i) for value in row] for i, row in enumerate(rows)]


def less_product(value, spread, lines):
    for f, line in zip(spread, lines):
        value = value - f * line
    return value


def forward(rows, steps):
    rows = [list(row) for row in rows]
    for first in range(0, steps, CHUNK):
        count = min(CHUNK, steps - first)
        own = range(first // 8, (first + count + 7) // 8)
        below = range(own.stop, len(rows))
        spread = {i: [lanes_of(rows[i][0], first + t) for t in range(count)] for i in below}
        solved = eliminate([rows[i] for i in own], first, count)
        for i, row in zip(own, solved):
            rows[i] = row
        for g in range(len(rows[0])):
            lines = [row_of(solved[t // 8][g], t % 8) for t in range(count)]
            for i in below:
                rows[i][g] = less_product(rows[i][g], spread[i], lines)
    return rows


def cosine_of(steps):
    quarter = (steps + 8) >> 4
    angle = (steps - 16 * quarter).astype(jnp.float32) * (2.0 * math.pi / PHASE_LEVELS)
    square = angle * angle
    cosine = 1.0 + square * (
        -1 / 2 + square * (1 / 24 + square * (-1 / 720 + square * (1 / 40320 - square / 3628800)))
    )
    sine = angle * (
        1.0 + square * (-1 / 6 + square * (1 / 120 + square * (-1 / 5040 + square / 362880)))
    )
    value = jnp.where((quarter & 1) == 0, cosine, sine)
    return jnp.where(((quarter + 1) & 2) == 0, value, -value)


def identity_kernel(out_ref):
    row = lax.broadcasted_iota(jnp.int32, (64, 128), 0)
    column = lax.broadcasted_iota(jnp.int32, (64, 128), 1) & 63
    source = jnp.where(column < 62, column // 2 + 31 * (column & 1), 64)
    out_ref[...] = jnp.where(row == source, 1.0, 0.0)


def message_kernel(_, samples_ref, codes_ref, panel_codes_ref, loading_ref, out_ref, side_ref):
    side_ref[0:1, :] = cosine_of(panel_codes_ref[...])
    side_ref[1:2, :] = cosine_of(panel_codes_ref[...] - 16)
    own = lax.broadcasted_iota(jnp.int32, (1, 8), 1) == lax.axis_index("tile_y")
    load = jnp.sum(jnp.where(own, loading_ref[...], 0.0), axis=1, keepdims=True)
    side_ref[2:8, :] = jnp.broadcast_to(load, (6, 128))
    codes = jnp.concatenate([codes_ref[...], jnp.zeros((8, 96), jnp.int32)], axis=1)
    row = lax.broadcasted_iota(jnp.int32, (8, 128), 0)
    lane = lax.broadcasted_iota(jnp.int32, (8, 128), 1)
    real = pltpu.roll(codes, 127, 1)
    imag = pltpu.roll(codes, 30, 1)
    last = pltpu.roll(codes, 62, 1)
    twin = pltpu.roll(codes, 63, 1)
    codes = jnp.where(lane < 31, real, jnp.where(lane < 62, imag, last))
    codes = jnp.where(lane == 63, twin, codes)
    imaginary = jnp.where((lane >= 31) & (lane != 62), 1, 0)

    def columns(first):
        spread = row_of(codes, first)
        for t in range(1, 4):
            spread = jnp.where(row >= 2 * t, row_of(codes, first + t), spread)
        return cosine_of(spread + 16 * (imaginary - (row & 1)))

    table = jnp.concatenate([columns(0), columns(4)], axis=0)
    table = (table / math.sqrt(256)).astype(jnp.bfloat16)
    for p in range(8):
        samples = samples_ref[p].reshape(16, SNAPS)
        for z in range(2):
            for b in range(4):
                out_ref[2 * p + z, 16 * b : 16 * b + 16, :] = samples[:, 128 * b : 128 * b + 128]
            out_ref[2 * p + z, 64:80, :] = table


def beams_kernel(got_ref, beams_ref):
    got = got_ref[...]
    table = got[:, 64:80, :].reshape(256, 128)
    samples = jnp.concatenate(
        [got[:, 16 * b : 16 * b + 16, :].reshape(256, 128) for b in range(4)], axis=1
    )
    beams_ref[...] = lax.dot_general(
        table, samples, (((0,), (0,)), ((), ())), preferred_element_type=jnp.float32
    )[:64]


def cancel_kernel(side_ref, identity_ref, beams_ref, out_ref):
    load = side_ref[2:3, 0:64]
    core = lax.axis_index("core")
    beams = beams_ref[0] + beams_ref[1]
    covar = square(beams) / SNAPS
    row = lax.broadcasted_iota(jnp.int32, (64, 64), 0)
    column = lax.broadcasted_iota(jnp.int32, (64, 64), 1)
    covar = covar + jnp.where(row == column, jnp.broadcast_to(load, (64, 64)), 0.0)
    covar = jnp.concatenate([covar, jnp.zeros((64, 64), jnp.float32)], axis=1)
    half = jnp.where(core == 0, beams[:, :256], beams[:, 256:])
    whole = jnp.concatenate([covar, half, identity_ref[...]], axis=1)
    rows = [
        [whole[8 * i : 8 * i + 8, 128 * g : 128 * g + 128] for g in range(4)] for i in range(8)
    ]
    last = forward(rows, 62)[7]
    lane = lax.broadcasted_iota(jnp.int32, (1, 128), 1)
    cancel = jnp.where(lane < 64, -last[3][6:7, :], -last[3][7:8, :])
    line = jnp.concatenate([last[1][6:8, :], last[2][6:8, :], cancel], axis=0)
    for i in range(8):
        out_ref[5 * i : 5 * i + 5, :] = line
    lines = out_ref[0:40, :]
    for i in range(1, 16):
        out_ref[40 * i : 40 * i + 40, :] = lines


def square(value):
    return lax.dot_general(
        value,
        value,
        (((1,), (1,)), ((), ())),
        precision=HIGHEST,
        preferred_element_type=jnp.float32,
    )


def split(value):
    high = value.astype(jnp.bfloat16)
    rest = value - high.astype(jnp.float32)
    middle = rest.astype(jnp.bfloat16)
    low = (rest - middle.astype(jnp.float32)).astype(jnp.bfloat16)
    return high, middle, low


def product(factor, solved, lane):
    width = solved.shape[1]

    def placed(part):
        parts = [part]
        if lane:
            parts = [jnp.zeros((lane, width), jnp.bfloat16)] + parts
        if lane + CHUNK < 128:
            parts = parts + [jnp.zeros((128 - lane - CHUNK, width), jnp.bfloat16)]
        return jnp.concatenate(parts, axis=0)

    high, middle, low = split(factor)
    upper, centre, lower = [placed(part) for part in split(solved)]

    def multiplied(left, right):
        return jnp.dot(
            jnp.concatenate(left, axis=1),
            jnp.concatenate(right, axis=0),
            preferred_element_type=jnp.float32,
        )

    return (
        multiplied((high, low), (lower, upper))
        + multiplied((high, middle), (centre, centre))
        + multiplied((high, middle), (upper, upper))
    )


def array_kernel(side_ref, lines_ref, cancel_ref, out_ref, work_ref):
    y = lax.axis_index("tile_y")
    cancel = lines_ref[pl.ds(lax.axis_index("panel") * 40 + 4, 8, stride=5), :]
    cancel_ref[:, 0, :] = cancel[:, :62]
    cancel_ref[:, 1, :] = pltpu.roll(cancel, 64, 1)[:, :62]

    blocks = [
        [lines_ref[pl.ds(640 * h + 2 * b + k, 128, stride=5), :] for h in range(2) for b in range(2)]
        for k in range(2)
    ]
    flat = jnp.concatenate([jnp.concatenate(row, axis=1) for row in blocks], axis=0)
    row = lax.broadcasted_iota(jnp.int32, (256, 256), 0)
    column = lax.broadcasted_iota(jnp.int32, (256, 256), 1)
    work_ref[0:256, 0:256] = square(flat) / SNAPS + jnp.where(row == column, ARRAY_LOAD, 0.0)

    cosine = side_ref[0:1, :]
    sine = side_ref[1:2, :]
    spread_cosine = jnp.broadcast_to(cosine, (128, 128)).T
    spread_sine = jnp.broadcast_to(sine, (128, 128)).T
    block = y // 2
    slot = (y % 2) * 4 + lax.axis_index("tile_z") * 2 + lax.axis_index("core")
    mine = jnp.where(
        block < 2,
        jnp.where(block == 0, flat[:, 0:128], flat[:, 128:256]),
        jnp.where(block == 2, flat[:, 256:384], flat[:, 384:512]),
    )
    mine = pltpu.roll(mine, lax.rem(128 - 16 * slot, 128), 1)
    lane = lax.broadcasted_iota(jnp.int32, (128, 128), 1)

    def right_side(values, first, second):
        values = jnp.where(lane < 16, values, 0.0)
        return jnp.where(lane == 16, first, jnp.where(lane == 17, second, values))

    work_ref[0:128, 256:384] = right_side(mine[:128], spread_cosine, -spread_sine)
    work_ref[128:256, 256:384] = right_side(mine[128:], spread_sine, spread_cosine)
    work_ref[256:ROWS, :] = jnp.zeros((ROWS - 256, 384), jnp.float32)
    work_ref[256:257, 0:128] = cosine
    work_ref[256:257, 128:256] = sine
    work_ref[257:258, 0:128] = -sine
    work_ref[257:258, 128:256] = cosine

    for base in range(0, 256, CHUNK):
        stop = base + CHUNK
        first = base // 128
        lane = base % 128
        groups = [0, 1, 2] if base < MOVE else [first, 1 - first]
        after = [g for g in groups if base < MOVE or g == 0 or stop < 256]
        near = min(stop + NEAR, ROWS) if stop < 256 else 264
        rows = [
            [work_ref[r : r + 8, 128 * g : 128 * g + 128] for g in groups]
            for r in range(base, stop, 8)
        ]
        spread = {
            r: [
                lanes_of(work_ref[r : r + 8, 128 * first : 128 * first + 128], lane + t)
                for t in range(CHUNK)
            ]
            for r in range(stop, near, 8)
        }
        rows = eliminate(rows, lane, CHUNK)
        rows = [[row[groups.index(g)] for g in after] for row in rows]
        for i, g in enumerate(after):
            lines = [row_of(rows[t // 8][i], t % 8) for t in range(CHUNK)]
            span = slice(128 * g, 128 * g + 128)
            for r in range(stop, near, 8):
                work_ref[r : r + 8, span] = less_product(work_ref[r : r + 8, span], spread[r], lines)
        if near < ROWS:
            factor = work_ref[near:ROWS, 128 * first : 128 * first + 128]
            solved = jnp.concatenate([jnp.concatenate(row, axis=1) for row in rows], axis=0)
            delta = product(factor, solved, lane)
            for i, g in enumerate(after):
                span = slice(128 * g, 128 * g + 128)
                work_ref[near:ROWS, span] = work_ref[near:ROWS, span] - delta[:, 128 * i : 128 * i + 128]
        if stop == MOVE:
            moved = lax.broadcasted_iota(jnp.int32, (8, 128), 1) < 18
            for r in range(stop, ROWS, 8):
                work_ref[r : r + 8, 0:128] = jnp.where(
                    moved, work_ref[r : r + 8, 256:384], work_ref[r : r + 8, 0:128]
                )

    final = -work_ref[256:264, 0:128]
    upper = row_of(final, 0)
    lower = row_of(final, 1)
    g00 = lanes_of(upper, 16)
    g01 = lanes_of(upper, 17)
    g10 = lanes_of(lower, 16)
    g11 = lanes_of(lower, 17)
    scale = math.sqrt(128.0) / (g00 * g11 - g01 * g10)
    first_row = (g11 * upper - g10 * lower) * scale
    second_row = (g00 * lower - g01 * upper) * scale
    place = lax.broadcasted_iota(jnp.int32, (8, 128), 0)
    out_ref[...] = jnp.where(place == 0, first_row, second_row)[0:2, 0:16]


def body(snapshots, beam_codes, panel_codes, loading):
    identity = pl.pallas_call(
        identity_kernel,
        out_shape=jax.ShapeDtypeStruct((64, 128), jnp.float32),
        out_specs=vmem(),
        compiler_params=limit(4),
        cost_estimate=pl.CostEstimate(
            flops=2000000000, bytes_accessed=4000000, transcendentals=0
        ),
        name="identity",
    )()
    message, side = pl.pallas_call(
        message_kernel,
        out_shape=(
            jax.ShapeDtypeStruct((16, 80, 128), jnp.bfloat16),
            jax.ShapeDtypeStruct((8, 128), jnp.float32),
        ),
        in_specs=[vmem()] * 5,
        out_specs=(vmem(), vmem()),
        compiler_params=limit(4),
        name="message",
    )(
        identity,
        snapshots,
        beam_codes.T,
        panel_codes.reshape(1, 128),
        loading.reshape(1, 8),
    )
    got = lax.all_to_all(message, ("tile_y", "tile_z"), 0, 0, tiled=True)
    beams = pl.pallas_call(
        beams_kernel,
        out_shape=jax.ShapeDtypeStruct((64, SNAPS), jnp.float32),
        in_specs=[vmem()],
        out_specs=vmem(),
        compiler_params=limit(4),
        name="beams",
    )(got)
    beams = lax.all_gather(beams, "core")
    lines = pl.pallas_call(
        cancel_kernel,
        out_shape=jax.ShapeDtypeStruct((640, 128), jnp.float32),
        in_specs=[vmem(), vmem(), vmem()],
        out_specs=vmem(),
        compiler_params=limit(4),
        name="cancel",
    )(side, identity, beams)
    lines = lines.reshape(128, 5, 1, 128)
    gathered = lax.all_to_all(lines, ("panel", "tile_y"), 0, 0, tiled=True)
    gathered = lax.all_gather(gathered.reshape(640, 128), "core", tiled=True)
    cancel, beam_out = pl.pallas_call(
        array_kernel,
        out_shape=(
            jax.ShapeDtypeStruct((8, 2, 62), jnp.float32),
            jax.ShapeDtypeStruct((2, 16), jnp.float32),
        ),
        in_specs=[vmem(), vmem()],
        out_specs=(vmem(), vmem()),
        scratch_shapes=[pltpu.VMEM((ROWS, 384), jnp.float32)],
        compiler_params=limit(8),
        name="array",
    )(side, gathered)
    return cancel.transpose(0, 2, 1), beam_out


def solution(mesh):
    torus = Mesh(
        mesh.devices.reshape(mesh.shape["panel"], 8, 2, 2), ("panel", "tile_y", "tile_z", "core")
    )
    return jax.shard_map(
        body,
        mesh=torus,
        in_specs=(P("panel", TILE, None, None), P(None, TILE), P(), P("panel")),
        out_specs=(P("panel", None, None), P(None, TILE)),
        check_vma=False,
    )
```
